128 devices in a mesh: ctx: 8 (over y_hi, z), exp: 16 (over y_lo, x, core).
Axes of the slice: x: 4, y: 4 (y_hi: 2, y_lo: 2; y = y_hi * 2 + y_lo), z: 4, core: 2. Of those that a mesh axis runs over, the one named last changes fastest.
Arguments:
- queries: bfloat16 [1024, 64, 576], P('ctx', 'exp'), may hold values from -16 to 16
- prior_codes: bfloat16 [3072, 576], P('ctx'), may hold values from -4 to 4
- fresh_codes: bfloat16 [1024, 576], P('ctx'), may hold values from -4 to 4
- prior_powers: int32 [24], P('ctx'), may hold values from -1 to 1
- fresh_powers: int32 [8], P('ctx'), may hold values from -1 to 1
- block_mask: int32 [8, 32], replicated, may hold values from 0 to 1, as said below
- value_up: bfloat16 [64, 512, 128], P('exp'), may hold values from -0.25 to 0.25
- output_weight: bfloat16 [8192, 7168], P('exp'), may hold values from -0.0625 to 0.0625
- residual: bfloat16 [1024, 7168], P(('ctx', 'exp')), may hold values from -2 to 2
- norm_gain: bfloat16 [7168], replicated, may hold values from 0.5 to 1.5
- router: bfloat16 [7168, 16], replicated, may hold values from -0.0625 to 0.0625
- route_ids: int32 [1024, 2], P(('ctx', 'exp')), may hold values from 0 to 15, all different within a row; in each aligned block of 8 rows (0 to 7, 8 to 15, ...) at most 2 rows name the same one
- gate_weight: bfloat16 [16, 7168, 2048], P('exp', None, 'ctx'), may hold values from -0.0625 to 0.0625
- up_weight: bfloat16 [16, 7168, 2048], P('exp', None, 'ctx'), may hold values from -0.0625 to 0.0625
- down_weight: bfloat16 [16, 2048, 7168], P('exp', 'ctx'), may hold values from -0.125 to 0.125
Outputs:
- layer_out: bfloat16 [1024, 7168], P(('ctx', 'exp'))
The draws below stay inside these ranges and needn't reach their ends.
Inputs may be any that keep to these rules, and one draw needn't show every extreme that they name: block_mask[q, k] is 1 exactly when key block k (the prior blocks first, then the new ones) lies in the same document as new block q and not after it; every new block sees itself. `route_ids`: the 8 tokens of one device name one expert at most 2 times in all.
All inputs are finite; a program needn't handle non-finite values.
Results may differ from the reference program's by a relative error of at most 0.034.
Values may be sent and summed in bfloat16 or wider, within the bound.
No kernel may reach another device: no remote copies, remote signals or barrier semaphores. Data moves between devices by JAX's collectives and lax.ppermute only.
A program may use at most 128 MiB of HBM per device.

```python
import math
import jax
import jax.numpy as jnp
import numpy as np
from jax import lax

D = 7168
LATENT = 512
ROPE = 64
NOPE = 128
VHEAD = 128
FF = 2048
HEAD_DEV = 4
ROUTES = 2
TOK_DEV = 8
PB = 3
HEADS = 64
EXPERTS = 16
CAP = 2
FRESH = 1024
PRIOR = 3072
N_CTX = 8
N_EXP = 16


def shared_codes(key, reach):
    raw = jax.random.normal(key, (TOK_DEV * N_EXP * N_CTX, LATENT + ROPE), jnp.float32)
    return jnp.clip(raw, -reach, reach)


def draw_fresh_codes(key, part):
    code_rows = shared_codes(key, 4.0)
    return code_rows.astype(jnp.bfloat16)


def draw_queries(key, part):
    shape = (TOK_DEV * N_EXP * N_CTX, HEAD_DEV * N_EXP, LATENT + ROPE)
    key = jax.random.fold_in(key, 7)
    result = jnp.clip(jax.random.normal(key, shape, jnp.float32), -4.0, 4.0)
    return result.astype(jnp.bfloat16)


def draw_prior_powers(key, part):
    key = jax.random.fold_in(key, 13)
    first_key, second_key = jax.random.split(key)
    count = PB * N_CTX
    values = jax.random.randint(first_key, (count,), -1, 2)
    step = jax.random.randint(second_key, (), 1, 3)
    other = (values[count - 1] + 1 + step) % 3 - 1
    return values.at[0].set(other).astype(jnp.int32)


def draw_block_mask(key, part):
    key = jax.random.fold_in(key, 5)
    first_key, second_key = jax.random.split(key)
    block_total = (PB + 1) * N_CTX
    first_new = PB * N_CTX
    start_block = jax.random.randint(first_key, (), 0, first_new + 1)
    fresh_starts = jax.random.randint(second_key, (block_total,), 0, 2)
    key_block = jnp.arange(block_total)
    starts = jnp.where(key_block == start_block, 1, jnp.where(key_block > first_new, fresh_starts, 0))
    document = jnp.cumsum(starts)
    query_block = first_new + jnp.arange(N_CTX)
    same_doc = document[None, :] == document[query_block][:, None]
    return jnp.logical_and(same_doc, key_block[None, :] <= query_block[:, None]).astype(jnp.int32)


def plant(array, key, least, top_value):
    longest = array.shape.index(max(array.shape))
    spots = []
    for shift in (0, 1):
        where = [jax.random.randint(jax.random.fold_in(key, axis), (), 0, length) for axis, length in enumerate(array.shape)]
        where[longest] = (where[longest] + shift) % array.shape[longest]
        spots.append(tuple(where))
    return array.at[spots[0]].set(least).at[spots[1]].set(top_value)


def level_of(key, dims, cuts, smallest, largest):
    level = 1.0
    for axis_at, parts in cuts:
        steps = jax.random.uniform(jax.random.fold_in(jax.random.fold_in(key, 6), axis_at), (parts,), jnp.float32, smallest / len(cuts), largest / len(cuts))
        level = level * jnp.repeat(jnp.exp(steps), dims[axis_at] // parts).reshape((-1,) + (1,) * (len(dims) - 1 - axis_at))
    return level


def shared_out(stream_key, own, number, rows, number_of, top, most, lean):
    ranking = jax.random.permutation(stream_key, number_of)
    crowded, common = shares(number_of, rows * top, most, lean, True), shares(number_of, rows * top, most, lean, False)
    places = jnp.arange(number_of)

    def named(tallies, offset_by):
        used = int((tallies > 0).sum())
        fixed = max(1, used // 4)
        moved = fixed + (places - fixed + offset_by * (used - fixed)) % max(1, number_of - fixed)
        return jnp.zeros((number_of,), jnp.int32).at[ranking[jnp.where(places < fixed, places, moved)]].set(jnp.asarray(tallies, jnp.int32))

    tallies = jnp.where(number % 4 == 0, named(crowded, number // 4), named(common, number - number // 4 - 1))
    mixed = jax.random.permutation(jax.random.fold_in(own, 3), number_of)
    giver, receiver = mixed[0:number_of // 2 * 2:2], mixed[1:number_of // 2 * 2:2]
    margin = jnp.minimum(tallies[giver] - 1, most - tallies[receiver]) // 2
    margin = jnp.where((giver == ranking[0]) | (receiver == ranking[0]) | (tallies[receiver] == 0), 0, jnp.maximum(margin, 0))
    moved = jax.random.randint(jax.random.fold_in(own, 4), (number_of // 2,), 0, 1 << 20) % (margin + 1)
    tallies = tallies.at[giver].add(-moved).at[receiver].add(moved)
    labels = jnp.searchsorted(jnp.cumsum(tallies), jnp.arange(rows * top), side="right").astype(jnp.int32)
    table = labels.reshape(top, rows).T
    table = table[jax.random.permutation(jax.random.fold_in(own, 1), rows)]
    offset_by = jax.random.randint(jax.random.fold_in(own, 2), (rows, 1), 0, top)
    return jnp.take_along_axis(table, (jnp.arange(top)[None, :] + offset_by) % top, axis=1)


def shares(amount, total, limit, skew, full):
    loads = [(1 << 20) // math.isqrt(rank ** skew) + 1 for rank in range(1, amount + 1)]
    largest = limit if full else min(limit, max(-(-total // amount), total * loads[0] // sum(loads)))
    least = 1 if total - largest >= amount - 1 else 0
    counts, rest = [largest] + [least] * (amount - 1), total - largest - least * (amount - 1)
    while rest > 0:
        movable = [i for i in range(1, amount) if counts[i] < largest] or [i for i in range(1, amount) if counts[i] < limit]
        pool, left = sum([loads[i] for i in movable]), rest
        for i in movable:
            extra = min(limit - counts[i], max(1, left * loads[i] // pool), rest)
            counts[i] = counts[i] + extra
            rest = rest - extra
    return np.array(counts)


def scatter_about(key, dims, spread, limit, cuts=(), dtype=jnp.bfloat16):
    factor_of = level_of(key, dims, cuts, -0.22, 0.18) if cuts else 1.0
    entries = jax.random.normal(key, dims, jnp.float32) * spread * factor_of
    return jnp.minimum(jnp.maximum(entries, -limit), limit).astype(dtype)


def setup_inputs(seed: int = 0) -> dict:
    seeds = jax.random.split(jax.random.key(seed), 16)
    queries = draw_queries(jax.random.fold_in(seeds[15], 71), 0)
    prior_codes = scatter_about(seeds[1], (PRIOR, LATENT + ROPE), 1.0, 4.0, ((0, 8),))
    fresh_codes = draw_fresh_codes(jax.random.fold_in(seeds[15], 71), 0)
    prior_powers = draw_prior_powers(jax.random.fold_in(seeds[15], 71), 0)
    fresh_powers = plant(jax.random.randint(seeds[4], (N_CTX,), -1, 2), jax.random.fold_in(seeds[4], 1), -1, 1).astype(jnp.int32)
    block_mask = draw_block_mask(jax.random.fold_in(seeds[15], 71), 0)
    value_up = scatter_about(seeds[6], (HEADS, LATENT, VHEAD), LATENT ** -0.5, 0.25, ((0, 16),))
    output_weight = scatter_about(seeds[7], (HEADS * VHEAD, D), (HEADS * VHEAD) ** -0.5, 0.0625, ((0, 16),))
    residual = scatter_about(seeds[8], (FRESH, D), 0.3, 2.0, ((0, 128),))
    norm_gain = jnp.clip(1.0 + 0.1 * jax.random.normal(seeds[9], (D,), jnp.float32), 0.5, 1.5).astype(jnp.bfloat16)
    router = scatter_about(seeds[10], (D, EXPERTS), D ** -0.5, 0.0625)
    route_ids_keys = jax.random.split(jax.random.fold_in(seeds[11], 1), FRESH // TOK_DEV)
    route_ids_turns = jax.random.permutation(jax.random.fold_in(seeds[11], 3), FRESH // TOK_DEV)
    route_ids = jax.vmap(lambda own, number: shared_out(jax.random.fold_in(seeds[11], 2), own, number, TOK_DEV, EXPERTS, ROUTES, CAP, 2))(route_ids_keys, route_ids_turns).reshape((FRESH, ROUTES))
    gate_weight = scatter_about(seeds[12], (EXPERTS, D, FF), D ** -0.5, 0.0625, ((0, 16), (2, 8)))
    up_weight = scatter_about(seeds[13], (EXPERTS, D, FF), D ** -0.5, 0.0625, ((0, 16), (2, 8)))
    down_weight = scatter_about(seeds[14], (EXPERTS, FF, D), FF ** -0.5, 0.125, ((0, 16), (1, 8)))
    return {"queries": queries, "prior_codes": prior_codes, "fresh_codes": fresh_codes, "prior_powers": prior_powers, "fresh_powers": fresh_powers, "block_mask": block_mask, "value_up": value_up, "output_weight": output_weight, "residual": residual, "norm_gain": norm_gain, "router": router, "route_ids": route_ids, "gate_weight": gate_weight, "up_weight": up_weight, "down_weight": down_weight}


def power_two(powers):
    return jnp.where(powers < 0, 0.5, jnp.where(powers > 0, 2.0, 1.0)).astype(jnp.float32)

def reference(queries, prior_codes, fresh_codes, prior_powers, fresh_powers, block_mask, value_up, output_weight, residual, norm_gain, router, route_ids, gate_weight, up_weight, down_weight):
    rows_block = TOK_DEV * N_EXP
    fresh_total = rows_block * N_CTX
    prior_total = PB * rows_block * N_CTX
    key_total = prior_total + fresh_total
    prior_scale = jnp.repeat(power_two(prior_powers), rows_block)
    fresh_scale = jnp.repeat(power_two(fresh_powers), rows_block)
    latent = jnp.concatenate([prior_codes.astype(jnp.float32) * prior_scale[:, None], fresh_codes.astype(jnp.float32) * fresh_scale[:, None]], axis=0).astype(jnp.bfloat16)
    query_block = jnp.arange(fresh_total) // rows_block
    key_block = jnp.arange(key_total) // rows_block
    allowed = block_mask[query_block[:, None], key_block[None, :]] > 0
    allowed = jnp.logical_and(allowed, jnp.arange(key_total)[None, :] <= prior_total + jnp.arange(fresh_total)[:, None])
    scale_factor = 1.0 / (NOPE + ROPE) ** 0.5

    def one_head(head_index):
        head_queries = queries[:, head_index, :]
        scores = jnp.dot(head_queries, latent.T, preferred_element_type=jnp.float32) * scale_factor
        scores = jnp.where(allowed, scores, -1e+30)
        row_top = lax.optimization_barrier(jnp.max(scores, axis=1, keepdims=True))
        weights = jnp.where(allowed, jnp.exp(scores - row_top), 0.0)
        row_total = lax.optimization_barrier(jnp.sum(weights, axis=1, keepdims=True))
        mixture = jnp.dot(weights.astype(jnp.bfloat16), latent[:, :LATENT], preferred_element_type=jnp.float32)
        attended = (mixture / row_total).astype(jnp.bfloat16)
        return jnp.dot(attended, value_up[head_index], preferred_element_type=jnp.float32).astype(jnp.bfloat16)
    heads_out = lax.map(one_head, jnp.arange(HEADS))
    head_dev = HEADS // N_EXP
    grouped = heads_out.reshape(N_EXP, head_dev, fresh_total, VHEAD).transpose(0, 2, 1, 3).reshape(N_EXP, fresh_total, head_dev * VHEAD)
    out_groups = output_weight.reshape(N_EXP, head_dev * VHEAD, D)

    def group_step(running, pair):
        group_rows, group_weight = pair
        rounded = jnp.dot(group_rows, group_weight, preferred_element_type=jnp.float32).astype(jnp.bfloat16)
        rounded = lax.optimization_barrier(rounded)
        return (running + rounded.astype(jnp.float32), None)
    attention, unused = lax.scan(group_step, jnp.zeros((fresh_total, D), jnp.float32), (grouped, out_groups))
    hidden = (residual.astype(jnp.float32) + attention).astype(jnp.bfloat16)
    hidden_wide = hidden.astype(jnp.float32)
    normed = (hidden_wide * lax.rsqrt(lax.optimization_barrier(jnp.mean(hidden_wide * hidden_wide, axis=1, keepdims=True)) + 1e-06) * norm_gain.astype(jnp.float32)).astype(jnp.bfloat16)
    affinity = jax.nn.sigmoid(jnp.dot(normed, router, preferred_element_type=jnp.float32))
    route_hits = route_ids[:, :, None] == jnp.arange(EXPERTS)[None, None, :]
    chosen = lax.optimization_barrier(jnp.sum(jnp.where(route_hits, affinity[:, None, :], 0.0), axis=2))
    gate_values = 2.5 * chosen / lax.optimization_barrier(jnp.sum(chosen, axis=1, keepdims=True))
    devices = N_CTX * N_EXP
    flat_ids = route_ids.reshape(devices, TOK_DEV * ROUTES)
    flat_hits = (flat_ids[:, :, None] == jnp.arange(EXPERTS)[None, None, :]).astype(jnp.int32)
    before = jnp.cumsum(flat_hits, axis=1) - flat_hits
    slot_index = lax.optimization_barrier(jnp.sum(before * flat_hits, axis=2))
    source = jnp.arange(devices)[:, None]
    position = (source * CAP + slot_index).astype(jnp.int32)
    token_of = (source * TOK_DEV + jnp.arange(TOK_DEV * ROUTES)[None, :] // ROUTES).astype(jnp.int32)
    slot_table = jnp.zeros((EXPERTS, devices * CAP), jnp.int32).at[flat_ids, position].set(token_of)
    slice_width = FF // N_CTX

    def one_expert(expert_index):
        token_rows = normed[slot_table[expert_index]]
        gate_proj = jnp.dot(token_rows, gate_weight[expert_index], preferred_element_type=jnp.float32)
        up_proj = jnp.dot(token_rows, up_weight[expert_index], preferred_element_type=jnp.float32)
        inner_act = (jax.nn.silu(gate_proj) * up_proj).astype(jnp.bfloat16)
        slice_acts = inner_act.reshape(-1, N_CTX, slice_width).transpose(1, 0, 2).astype(jnp.float32)
        down_slices = down_weight[expert_index].reshape(N_CTX, slice_width, D).astype(jnp.float32)
        slice_out = jnp.einsum('cnf,cfd->cnd', slice_acts, down_slices).astype(jnp.bfloat16)
        slice_out = lax.optimization_barrier(slice_out)
        return lax.optimization_barrier(jnp.sum(slice_out.astype(jnp.float32), axis=0)).astype(jnp.bfloat16)
    expert_out = lax.map(one_expert, jnp.arange(EXPERTS))
    routed = expert_out[flat_ids, position].reshape(fresh_total, ROUTES, D).astype(jnp.float32)
    expert_mix = lax.optimization_barrier(jnp.sum(gate_values[:, :, None] * routed, axis=1))
    return (hidden_wide + expert_mix).astype(jnp.bfloat16)
```

```python
import jax
import jax.numpy as jnp
from jax import lax
from jax.experimental import pallas as pl
from jax.experimental.pallas import tpu as pltpu
from jax.sharding import PartitionSpec as P

ROPE = 64
NOPE = 128
Y_HI, Z, Y_LO, X, CORES = 2, 4, 2, 4, 2
F32 = jnp.float32
BF16 = jnp.bfloat16


def ctx_pairs(move):
    return [
        (y * Z + z, move(y, z)[0] * Z + move(y, z)[1]) for y in range(Y_HI) for z in range(Z)
    ]


Z_UP = ctx_pairs(lambda y, z: (y, (z + 1) % Z))
Z_DOWN = ctx_pairs(lambda y, z: (y, (z - 1) % Z))
Y_SWAP = ctx_pairs(lambda y, z: (1 - y, z))
CORE_SWAP = [(i, i ^ 1) for i in range(Y_LO * X * CORES)]
SAME_CORE = [[2 * i + core for i in range(Y_LO * X)] for core in range(CORES)]


def over_ctx(value, pairs):
    return lax.ppermute(value, "ctx", pairs)


def core_swap(value):
    return lax.ppermute(value, "exp", CORE_SWAP)


def power_two(powers):
    return jnp.where(powers < 0, 0.5, jnp.where(powers > 0, 2.0, 1.0)).astype(jnp.float32)


def attention_kernel(
    live, queries, own, mine1, other1, mine2, other2, mine3, other3, value_up, weight_hbm,
    out_keep, out_send, scores, top, total, mixture, weight, weight_sem,
):
    copy = pltpu.make_async_copy(weight_hbm, weight, weight_sem)
    copy.start()
    rows = queries.shape[0]
    heads, latent_width, head_width = value_up.shape
    tokens = rows // heads
    unit = scores.shape[2]
    block = unit // 2
    parts = (own, mine1, other1, mine2, other2, mine3, other3)
    factor = 1.4426950408889634 / (NOPE + ROPE) ** 0.5
    top[...] = jnp.full_like(top, -1e30)
    total[...] = jnp.zeros_like(total)
    mixture[...] = jnp.zeros_like(mixture)

    def each_unit(body):
        first = 0
        for part in parts:
            count = part.shape[0] // unit
            if part is own:
                for u in range(count):
                    body(part, u, u, u == count - 1)
            else:
                def step(u, part=part, first=first):
                    body(part, u, first + u, False)
                pl.loop(0, count)(step)
            first += count

    def score(part, u, number, diagonal):
        live0, live1 = live[2 * number], live[2 * number + 1]

        @pl.when(live0 + live1 > 0)
        def _():
            keys = part[pl.ds(u * unit, unit), :]
            found = lax.dot_general(
                queries[...], keys, (((1,), (1,)), ((), ())), preferred_element_type=F32
            )
            column = lax.broadcasted_iota(jnp.int32, (1, unit), 1)
            column_live = jnp.where(column < block, live0, live1) > 0
            if diagonal:
                row = lax.broadcasted_iota(jnp.int32, (rows, 1), 0) % tokens
                relative = row // (tokens // 2)
                within = row % (tokens // 2)
                side = jnp.where(relative == 0, live[32], 1 - live[32])
                token = within // 8 * 16 + side * 8 + within % 8
                seen = jnp.logical_or(column < block, column - block <= token)
                allowed = jnp.logical_and(column_live, seen)
            else:
                allowed = column_live
            found = jnp.where(allowed, found, -1e30)
            scores[number] = found
            top[...] = jnp.maximum(top[...], found)

    def mix(part, u, number, diagonal):
        live0, live1 = live[2 * number], live[2 * number + 1]

        @pl.when(live0 + live1 > 0)
        def _():
            weights = jnp.exp2((scores[number] - row_top) * factor)
            total[...] += weights
            mixture[...] += jnp.dot(
                weights.astype(BF16),
                part[pl.ds(u * unit, unit), :latent_width],
                preferred_element_type=F32,
            )

    each_unit(score)
    row_top = jnp.max(top[...], axis=1, keepdims=True)
    each_unit(mix)
    row_total = jnp.sum(total[...], axis=1, keepdims=True)
    per_head = []
    for head in range(heads):
        span = slice(head * tokens, (head + 1) * tokens)
        attended = (mixture[span] / row_total[span]).astype(BF16)
        per_head.append(
            jnp.dot(attended, value_up[head], preferred_element_type=F32).astype(BF16)
        )
    flat_heads = jnp.concatenate(per_head, axis=1)
    copy.wait()
    width = 1024
    half = tokens // 2

    @pl.loop(0, weight.shape[1] // width)
    def _(step):
        columns = pl.ds(pl.multiple_of(step * width, width), width)
        term = jnp.dot(flat_heads, weight[:, columns], preferred_element_type=F32)
        out_keep[:, columns] = term[:half].astype(BF16)
        out_send[:, columns] = term[half:].astype(BF16)


def attention_call(live, queries, parts, value_up, output_weight):
    rows = queries.shape[0]
    tokens = rows // value_up.shape[0]
    width = output_weight.shape[1]
    key_total = sum(part.shape[0] for part in parts)
    unit = 256
    vmem = pl.BlockSpec(memory_space=pltpu.VMEM)
    out = jax.ShapeDtypeStruct((tokens // 2, width), BF16)
    return pl.pallas_call(
        attention_kernel,
        out_shape=(out, out),
        in_specs=[pl.BlockSpec(memory_space=pltpu.SMEM)]
        + [vmem] * (2 + len(parts))
        + [pl.BlockSpec(memory_space=pl.ANY)],
        out_specs=(vmem, vmem),
        scratch_shapes=[
            pltpu.VMEM((key_total // unit, rows, unit), F32),
            pltpu.VMEM((rows, unit), F32),
            pltpu.VMEM((rows, unit), F32),
            pltpu.VMEM((rows, value_up.shape[1]), F32),
            pltpu.VMEM(output_weight.shape, BF16),
            pltpu.SemaphoreType.DMA,
        ],
        compiler_params=pltpu.CompilerParams(vmem_limit_bytes=44 * 2**20),
        cost_estimate=pl.CostEstimate(
            flops=6 * 10**9, bytes_accessed=16 * 10**6, transcendentals=2 * 10**6
        ),
        name="attention",
    )(live, queries, *parts, value_up, output_weight)


def gather_codes(codes, core):
    rows = codes.shape[0]
    half = lax.dynamic_slice_in_dim(codes, core * (rows // 2), rows // 2, 0)
    quarter = rows // 4
    down = over_ctx(half, Z_UP)
    up = over_ctx(half, Z_DOWN)
    side = over_ctx(half, Y_SWAP)
    mine1 = jnp.concatenate([down, up, side], axis=0)
    other1 = core_swap(mine1)
    side_down = over_ctx(side, Z_UP)
    side_up = over_ctx(side, Z_DOWN)
    far_low = over_ctx(down[:quarter], Z_UP)
    far_high = over_ctx(up[quarter:], Z_DOWN)
    mine2 = jnp.concatenate([side_down, side_up, far_low, far_high], axis=0)
    other2 = core_swap(mine2)
    side_far_low = over_ctx(side_down[:quarter], Z_UP)
    side_far_high = over_ctx(side_up[quarter:], Z_DOWN)
    mine3 = jnp.concatenate([side_far_low, side_far_high], axis=0)
    other3 = core_swap(mine3)
    return (codes, mine1, other1, mine2, other2, mine3, other3)


def block_numbers(ctx_index, core, prior_blocks):
    y, z = ctx_index // Z, ctx_index % Z

    def owner(dy, dz):
        return (y + dy) % Y_HI * Z + (z + dz) % Z

    def numbers(dy, dz, side):
        index = owner(dy, dz)
        found = []
        for sub in range(2):
            place = side * 2 + sub
            found.append(
                jnp.where(
                    place < prior_blocks,
                    index * prior_blocks + place,
                    prior_blocks * Y_HI * Z + index,
                )
            )
        return found

    groups = (
        ((0, -1), (0, 1), (1, 0)),
        ((1, -1), (1, 1), (0, 2)),
        ((1, 2),),
    )
    found = numbers(0, 0, 0) + numbers(0, 0, 1)
    for group in groups:
        for side in (core, 1 - core):
            for dy, dz in group:
                found = found + numbers(dy, dz, side)
    return jnp.stack([jnp.asarray(f, jnp.int32) for f in found])


def experts_kernel(
    own, down, up, side, side_down, side_up, far_low, far_high, side_far_low, side_far_high,
    gate_hbm, up_hbm, down_hbm,
    o_own, o_down, o_up, o_side, o_side_down, o_side_up, o_far_low, o_far_high, o_sf_low, o_sf_high,
    rows, gate_weight, up_weight, down_weight, acc, sems,
):
    sources = (own, down, up, side, side_down, side_up, far_low, far_high, side_far_low, side_far_high)
    results = (o_own, o_down, o_up, o_side, o_side_down, o_side_up, o_far_low, o_far_high, o_sf_low, o_sf_high)
    weight_copies = [
        pltpu.make_async_copy(source.at[0], target, sems.at[i])
        for i, (source, target) in enumerate(
            ((gate_hbm, gate_weight), (up_hbm, up_weight), (down_hbm, down_weight))
        )
    ]
    for copy in weight_copies:
        copy.start()
    starts = []
    at = 0
    for source in sources:
        starts.append(at)
        rows[at : at + source.shape[0], :] = source[...]
        at += source.shape[0]
    weight_copies[0].wait()
    gate_proj = jnp.dot(rows[...], gate_weight[...], preferred_element_type=F32)
    weight_copies[1].wait()
    up_proj = jnp.dot(rows[...], up_weight[...], preferred_element_type=F32)
    inner_act = (gate_proj / (1.0 + jnp.exp(-gate_proj)) * up_proj).astype(BF16)
    weight_copies[2].wait()
    width = 1024

    @pl.loop(0, down_weight.shape[1] // width)
    def _(step):
        columns = pl.ds(pl.multiple_of(step * width, width), width)
        term = jnp.dot(inner_act, down_weight[:, columns], preferred_element_type=F32)
        for start, result in zip(starts, results):
            result[:, columns] = term[start : start + result.shape[0]].astype(BF16)


def experts_call(blocks, gate_weight, up_weight, down_weight):
    vmem = pl.BlockSpec(memory_space=pltpu.VMEM)
    anywhere = pl.BlockSpec(memory_space=pl.ANY)
    row_count = sum(block.shape[0] for block in blocks)
    return pl.pallas_call(
        experts_kernel,
        out_shape=tuple(jax.ShapeDtypeStruct(block.shape, BF16) for block in blocks),
        in_specs=[vmem] * len(blocks) + [anywhere] * 3,
        out_specs=tuple([vmem] * len(blocks)),
        scratch_shapes=[
            pltpu.VMEM((row_count, blocks[0].shape[1]), BF16),
            pltpu.VMEM(gate_weight.shape[1:], BF16),
            pltpu.VMEM(up_weight.shape[1:], BF16),
            pltpu.VMEM(down_weight.shape[1:], BF16),
            pltpu.VMEM((8, 128), F32),
            pltpu.SemaphoreType.DMA((3,)),
        ],
        compiler_params=pltpu.CompilerParams(vmem_limit_bytes=44 * 2**20),
        cost_estimate=pl.CostEstimate(
            flops=3 * 10**9, bytes_accessed=19 * 10**6, transcendentals=65536
        ),
        name="experts",
    )(*blocks, gate_weight, up_weight, down_weight)


def gather_rows(own):
    half = own.shape[0] // 2
    down = over_ctx(own, Z_UP)
    up = over_ctx(own, Z_DOWN)
    side = over_ctx(own, Y_SWAP)
    side_down = over_ctx(side, Z_UP)
    side_up = over_ctx(side, Z_DOWN)
    far_low = over_ctx(down[:half], Z_UP)
    far_high = over_ctx(up[half:], Z_DOWN)
    side_far_low = over_ctx(side_down[:half], Z_UP)
    side_far_high = over_ctx(side_up[half:], Z_DOWN)
    return (own, down, up, side, side_down, side_up, far_low, far_high, side_far_low, side_far_high)


def added(*terms):
    total = terms[0].astype(F32)
    for term in terms[1:]:
        total = total + term.astype(F32)
    return total.astype(BF16)


def reduce_rows(blocks):
    own, down, up, side, side_down, side_up, far_low, far_high, sf_low, sf_high = blocks
    half = own.shape[0] // 2

    def add_half(block, low=None, high=None):
        first, second = block[:half], block[half:]
        if low is not None:
            first = added(first, low)
        if high is not None:
            second = added(second, high)
        return jnp.concatenate([first, second], axis=0)

    sf_low_in = over_ctx(sf_low, Z_UP)
    sf_high_in = over_ctx(sf_high, Z_DOWN)
    side_up = add_half(side_up, low=sf_low_in)
    side_down = add_half(side_down, high=sf_high_in)
    far_low_in = over_ctx(far_low, Z_UP)
    far_high_in = over_ctx(far_high, Z_DOWN)
    side_up_in = over_ctx(side_up, Z_UP)
    side_down_in = over_ctx(side_down, Z_DOWN)
    up = add_half(up, low=far_low_in)
    down = add_half(down, high=far_high_in)
    side = added(side, side_up_in, side_down_in)
    side_in = over_ctx(side, Y_SWAP)
    up_in = over_ctx(up, Z_UP)
    down_in = over_ctx(down, Z_DOWN)
    return added(own, up_in, down_in, side_in)


def on_device(
    queries,
    prior_codes,
    fresh_codes,
    prior_powers,
    fresh_powers,
    block_mask,
    value_up,
    output_weight,
    residual,
    norm_gain,
    router,
    route_ids,
    gate_weight,
    up_weight,
    down_weight,
):
    ctx_index = lax.axis_index("ctx")
    core = lax.axis_index("exp") % CORES
    rows_block, head_count, key_width = queries.shape
    prior_blocks = prior_powers.shape[0]
    scales = power_two(jnp.concatenate([prior_powers, fresh_powers], axis=0))
    codes = jnp.concatenate([prior_codes, fresh_codes], axis=0).astype(F32)
    codes = (codes * jnp.repeat(scales, rows_block)[:, None]).astype(BF16)
    parts = gather_codes(codes, core)

    mask_row = lax.dynamic_index_in_dim(block_mask, ctx_index, 0, keepdims=False)
    numbers = block_numbers(ctx_index, core, prior_blocks)
    chosen_blocks = numbers[:, None] == jnp.arange(mask_row.shape[0])[None, :]
    live = jnp.sum(jnp.where(chosen_blocks, mask_row[None, :], 0), axis=1)
    live = jnp.concatenate([live, core[None]]).astype(jnp.int32)
    groups = rows_block // 16
    split = queries.reshape(groups, 2, 8, head_count, key_width)
    first = jnp.where(core == 0, split[:, 0], split[:, 1])
    second = jnp.where(core == 0, split[:, 1], split[:, 0])
    ordered = jnp.stack([first, second], axis=0)
    ordered = jnp.transpose(ordered, (3, 0, 1, 2, 4)).reshape(head_count * rows_block, key_width)

    keep, send = attention_call(live, ordered, parts, value_up, output_weight)
    paired = added(keep, core_swap(send))
    model_width = residual.shape[1]
    pieces = lax.all_to_all(
        paired.reshape(groups, 8, model_width),
        "exp",
        split_axis=0,
        concat_axis=0,
        tiled=True,
        axis_index_groups=SAME_CORE,
    )
    attention = jnp.sum(pieces.astype(F32), axis=0)
    hidden = (residual.astype(F32) + attention).astype(BF16)
    hidden_wide = hidden.astype(F32)
    normed = (
        hidden_wide
        * lax.rsqrt(jnp.mean(hidden_wide * hidden_wide, axis=1, keepdims=True) + 1e-06)
        * norm_gain.astype(F32)
    ).astype(BF16)
    expert_count = router.shape[1]
    token_count, route_count = route_ids.shape
    capacity = token_count * route_count * 2 // expert_count
    affinity = jax.nn.sigmoid(jnp.dot(normed, router, preferred_element_type=F32))
    route_hits = route_ids[:, :, None] == jnp.arange(expert_count)[None, None, :]
    chosen = jnp.sum(jnp.where(route_hits, affinity[:, None, :], 0.0), axis=2)
    gate_values = 2.5 * chosen / jnp.sum(chosen, axis=1, keepdims=True)
    flat_hits = route_hits.reshape(token_count * route_count, expert_count).astype(jnp.int32)
    before = jnp.cumsum(flat_hits, axis=0) - flat_hits
    slot_index = jnp.sum(before * flat_hits, axis=1)
    target = route_ids.reshape(-1) * capacity + slot_index
    placing = (target[None, :] == jnp.arange(expert_count * capacity)[:, None]).astype(BF16)
    repeated = jnp.repeat(normed, route_count, axis=0)
    buffer = jnp.dot(placing, repeated, preferred_element_type=F32).astype(BF16)
    sectioned = lax.all_to_all(
        buffer.reshape(expert_count, capacity, model_width),
        "exp",
        split_axis=0,
        concat_axis=0,
        tiled=True,
    )
    blocks = gather_rows(sectioned.reshape(expert_count * capacity, model_width))
    partials = experts_call(blocks, gate_weight, up_weight, down_weight)
    summed = reduce_rows(partials)
    returned = lax.all_to_all(
        summed.reshape(expert_count, capacity, model_width),
        "exp",
        split_axis=0,
        concat_axis=0,
        tiled=True,
    ).reshape(expert_count * capacity, model_width)
    gathered_back = jnp.dot(
        jnp.transpose(placing), returned, preferred_element_type=F32
    ).reshape(token_count, route_count, model_width)
    expert_mix = jnp.sum(gate_values[:, :, None] * gathered_back, axis=1)
    return (hidden_wide + expert_mix).astype(BF16)


def solution(mesh):
    in_specs = (
        P("ctx", "exp", None),
        P("ctx", None),
        P("ctx", None),
        P("ctx"),
        P("ctx"),
        P(),
        P("exp", None, None),
        P("exp", None),
        P(("ctx", "exp"), None),
        P(),
        P(),
        P(("ctx", "exp"), None),
        P("exp", None, "ctx"),
        P("exp", None, "ctx"),
        P("exp", "ctx", None),
    )
    out_specs = P(("ctx", "exp"), None)
    return jax.shard_map(
        on_device, mesh=mesh, in_specs=in_specs, out_specs=out_specs, check_vma=False
    )
```

```python
import functools

import jax
import jax.numpy as jnp
from jax import lax
from jax.experimental import pallas as pl
from jax.experimental.pallas import tpu as pltpu
from jax.sharding import PartitionSpec as P

ROPE = 64
NOPE = 128
Y_HI, Z, Y_LO, X, CORES = 2, 4, 2, 4, 2
STEP_BLOCKS = 4
VMEM_LIMIT = 40 * 2**20
HEADS_HERE = 4
F32 = jnp.float32
BF16 = jnp.bfloat16


def ctx_pairs(move):
    pairs = []
    for y in range(Y_HI):
        for z in range(Z):
            for i in range(Y_LO * X * CORES):
                to_y, to_z = move(y, z, 1 - 2 * (i % CORES))
                pairs.append(
                    (
                        (y * Z + z) * Y_LO * X * CORES + i,
                        (to_y * Z + to_z) * Y_LO * X * CORES + i,
                    )
                )
    return pairs


AHEAD = ctx_pairs(lambda y, z, way: (y, (z + way) % Z))
BACK = ctx_pairs(lambda y, z, way: (y, (z - way) % Z))
ACROSS = ctx_pairs(lambda y, z, way: (1 - y, z))
CORE_SWAP = [(i, i ^ 1) for i in range(Y_LO * X * CORES)]
SAME_CORE = [[2 * i + core for i in range(Y_LO * X)] for core in range(CORES)]


def over_ctx(value, pairs):
    return lax.ppermute(value, ("ctx", "exp"), pairs)


def core_swap(value):
    return lax.ppermute(value, "exp", CORE_SWAP)


def power_two(powers):
    return jnp.where(powers < 0, 0.5, jnp.where(powers > 0, 2.0, 1.0)).astype(jnp.float32)


def attend(live, first_flag, queries, steps, diagonal, scores, top, total, mixture):
    rows = queries.shape[0]
    latent_width = mixture.shape[1]
    block = top.shape[1]
    factor = 1.4426950408889634 / (NOPE + ROPE) ** 0.5
    top[...] = jnp.full_like(top, -1e30)
    total[...] = jnp.zeros_like(total)
    mixture[...] = jnp.zeros_like(mixture)

    def keys_of(step, height):
        return jnp.concatenate([part[i, :height] for part, i in step], axis=1)

    def lane_fold(value, fold):
        folded = value[:, :block]
        for i in range(1, STEP_BLOCKS):
            folded = fold(folded, value[:, i * block : (i + 1) * block])
        return folded

    def flags_of(number):
        return [live[first_flag + STEP_BLOCKS * number + i] for i in range(STEP_BLOCKS)]

    def score(step, number):
        flags = flags_of(number)

        @pl.when(sum(flags) > 0)
        def _():
            found = jnp.dot(
                queries[...], keys_of(step, queries.shape[1]), preferred_element_type=F32
            )
            column = lax.broadcasted_iota(jnp.int32, (1, STEP_BLOCKS * block), 1) // block
            shown = jnp.zeros(column.shape, jnp.int32)
            for i, flag in enumerate(flags):
                shown = jnp.where(column == i, flag, shown)
            found = jnp.where(shown > 0, found, -1e30)
            if diagonal and number == 0:
                last = (STEP_BLOCKS - 1) * block
                seen = jnp.where(causal(), found[:, last:], -1e30)
                found = jnp.concatenate([found[:, :last], seen], axis=1)
            scores[number] = found
            top[...] = jnp.maximum(top[...], lane_fold(found, jnp.maximum))

    def causal():
        tokens = rows // HEADS_HERE
        row = lax.broadcasted_iota(jnp.int32, (rows, 1), 0) % tokens
        relative = row // (tokens // 2)
        within = row % (tokens // 2)
        side = jnp.where(relative == 0, live[live.shape[0] - 1], 1 - live[live.shape[0] - 1])
        token = within // 8 * 16 + side * 8 + within % 8
        return lax.broadcasted_iota(jnp.int32, (1, block), 1) <= token

    for number, step in enumerate(steps):
        score(step, number)
    row_top = jnp.max(top[...], axis=1, keepdims=True)

    def mix(step, number):
        @pl.when(sum(flags_of(number)) > 0)
        def _():
            weights = jnp.exp2((scores[number] - row_top) * factor)
            total[...] += lane_fold(weights, jnp.add)
            mixture[...] += lax.dot_general(
                weights.astype(BF16),
                keys_of(step, latent_width),
                (((1,), (1,)), ((), ())),
                preferred_element_type=F32,
            )

    for number, step in enumerate(steps):
        mix(step, number)
    return row_top


def near_kernel(
    live, queries, own, beside, beside_other, side, side_other, top, total, mixture, done, scores
):
    steps = [[(part, i) for i in range(STEP_BLOCKS)] for part in (own, beside, beside_other)]
    steps.append([(part, i) for part in (side, side_other) for i in range(STEP_BLOCKS // 2)])
    row_top = attend(live, 0, queries, steps, True, scores, top, total, mixture)
    top[...] = jnp.broadcast_to(row_top, top.shape)
    done[...] = jnp.ones_like(done)


def far_kernel(
    live, queries, beside, beside_other, far, far_other, side_far, side_far_other,
    near_top, near_total, near_mixture, value_up, weight_hbm,
    out_keep, out_send, scores, top, total, mixture, weight, weight_sem,
):
    copy = pltpu.make_async_copy(weight_hbm, weight, weight_sem)
    copy.start()
    heads = value_up.shape[0]
    tokens = queries.shape[0] // heads
    factor = 1.4426950408889634 / (NOPE + ROPE) ** 0.5
    steps = [[(part, i) for i in range(STEP_BLOCKS)] for part in (beside, beside_other)]
    for halves in ((far, far_other), (side_far, side_far_other)):
        steps.append([(part, i) for part in halves for i in range(STEP_BLOCKS // 2)])
    far_top = attend(
        live, 4 * STEP_BLOCKS, queries, steps, False, scores, top, total, mixture
    )
    near_row_top = near_top[:, :1]
    both_top = jnp.maximum(near_row_top, far_top)
    near_scale = jnp.exp2((near_row_top - both_top) * factor)
    far_scale = jnp.exp2((far_top - both_top) * factor)
    row_total = jnp.sum(near_total[...] * near_scale + total[...] * far_scale, axis=1, keepdims=True)
    near_scale = near_scale / row_total
    far_scale = far_scale / row_total
    per_head = []
    for head in range(heads):
        span = slice(head * tokens, (head + 1) * tokens)
        attended = near_mixture[span] * near_scale[span] + mixture[span] * far_scale[span]
        per_head.append(
            jnp.dot(
                attended.astype(BF16), value_up[head], preferred_element_type=F32
            ).astype(BF16)
        )
    flat_heads = jnp.concatenate(per_head, axis=1)
    copy.wait()
    out_width = 1024
    half = tokens // 2

    @pl.loop(0, weight.shape[1] // out_width)
    def _(step):
        columns = pl.ds(pl.multiple_of(step * out_width, out_width), out_width)
        term = jnp.dot(flat_heads, weight[:, columns], preferred_element_type=F32)
        out_keep[:, columns] = term[:half].astype(BF16)
        out_send[:, columns] = term[half:].astype(BF16)


def score_scratch(blocks, rows, block):
    return pltpu.VMEM((blocks // STEP_BLOCKS, rows, STEP_BLOCKS * block), F32)


def near_call(live, queries, near, value_up):
    rows, block = queries.shape[0], near[0].shape[2]
    vmem = pl.BlockSpec(memory_space=pltpu.VMEM)
    lanes = jax.ShapeDtypeStruct((rows, block), F32)
    return pl.pallas_call(
        near_kernel,
        out_shape=(
            lanes,
            lanes,
            jax.ShapeDtypeStruct((rows, value_up.shape[1]), F32),
            jax.ShapeDtypeStruct((8, block), F32),
        ),
        in_specs=[pl.BlockSpec(memory_space=pltpu.SMEM)] + [vmem] * (1 + len(near)),
        out_specs=(vmem,) * 4,
        scratch_shapes=[score_scratch(sum(part.shape[0] for part in near), rows, block)],
        compiler_params=pltpu.CompilerParams(vmem_limit_bytes=VMEM_LIMIT),
        cost_estimate=pl.CostEstimate(
            flops=3 * 10**9, bytes_accessed=6 * 10**6, transcendentals=10**6
        ),
        name="attention_near",
    )(live, queries, *near)


def far_call(live, queries, far, state, value_up, output_weight):
    rows, block = queries.shape[0], far[0].shape[2]
    tokens = rows // value_up.shape[0]
    vmem = pl.BlockSpec(memory_space=pltpu.VMEM)
    out = jax.ShapeDtypeStruct((tokens // 2, output_weight.shape[1]), BF16)
    return pl.pallas_call(
        far_kernel,
        out_shape=(out, out),
        in_specs=[pl.BlockSpec(memory_space=pltpu.SMEM)]
        + [vmem] * 11
        + [pl.BlockSpec(memory_space=pltpu.HBM)],
        out_specs=(vmem, vmem),
        scratch_shapes=[
            score_scratch(sum(part.shape[0] for part in far), rows, block),
            pltpu.VMEM((rows, block), F32),
            pltpu.VMEM((rows, block), F32),
            pltpu.VMEM((rows, value_up.shape[1]), F32),
            pltpu.VMEM(output_weight.shape, BF16),
            pltpu.SemaphoreType.DMA,
        ],
        compiler_params=pltpu.CompilerParams(vmem_limit_bytes=49 * 2**20),
        cost_estimate=pl.CostEstimate(
            flops=4 * 10**9, bytes_accessed=14 * 10**6, transcendentals=10**6
        ),
        name="attention_far",
    )(live, queries, *far, *state, value_up, output_weight)


def own_half(blocks, core):
    half_blocks = blocks.shape[0] // 2
    return lax.dynamic_slice_in_dim(blocks, core * half_blocks, half_blocks, 0)


def gather_codes(blocks, core):
    side = over_ctx(own_half(blocks, core), ACROSS)
    beside = over_ctx(blocks, AHEAD)
    beside_half = own_half(beside, core)
    far = over_ctx(beside_half, AHEAD)
    side_other, _ = lax.optimization_barrier((core_swap(side), beside_half))
    side_beside = over_ctx(jnp.concatenate([side, side_other], axis=0), AHEAD)
    side_far = over_ctx(far, ACROSS)
    near = (blocks, beside, core_swap(beside), side, side_other)

    def far_blocks(done):
        held = side_far * done[0, 0].astype(BF16)
        swapped = [core_swap(part) for part in (side_beside, far, held)]
        return (side_beside, swapped[0], far, swapped[1], held, swapped[2])

    return near, far_blocks


def block_flags(block_mask, ctx_index, core, prior_blocks):
    owners = block_mask.shape[0]
    mask_row = lax.dynamic_index_in_dim(block_mask, ctx_index, 0, keepdims=False)
    prior = mask_row[: owners * prior_blocks].reshape(owners, prior_blocks)
    fresh = mask_row[owners * prior_blocks :].reshape(owners, 1)
    flags = jnp.concatenate([prior, fresh], axis=1)
    half = flags.shape[1] // 2
    y, z = ctx_index // Z, ctx_index % Z
    way = 1 - 2 * core

    def of(dy, dz):
        owner = (y + dy) % Y_HI * Z + (z + dz) % Z
        return jnp.sum(jnp.where(jnp.arange(owners)[:, None] == owner, flags, 0), axis=0)

    def mine_first(found):
        return jnp.where(core == 0, found, jnp.roll(found, half))

    ordered = (
        of(0, 0),
        of(0, -way),
        of(0, way),
        mine_first(of(1, 0)),
        mine_first(of(1, -way)),
        jnp.roll(mine_first(of(1, way)), half),
        mine_first(of(0, 2)),
        mine_first(of(1, 2)),
    )
    return jnp.concatenate(ordered + (core[None],)).astype(jnp.int32)


def store_rows(results, columns, term):
    at = 0
    for result in results:
        result[:, columns] = term[at : at + result.shape[0]].astype(BF16)
        at += result.shape[0]


def experts_kernel(count, holds, *refs):
    sources, weights_in = refs[:count], refs[count : count + 3]
    results = refs[count + 3 : 2 * count + 3]
    if holds:
        gate_weight, up_weight, down_weight, rows, sems = refs[2 * count + 3 :]
    else:
        gate_weight, up_weight, down_weight = weights_in
        (rows,) = refs[2 * count + 3 :]
    cuts = 4
    depth = rows.shape[1] // cuts
    width = depth // 2

    def weight_copy(kind, cut):
        span = slice(cut * depth, (cut + 1) * depth)
        source, target = weights_in[kind], (gate_weight, up_weight, down_weight)[kind]
        if kind == 2:
            return pltpu.make_async_copy(
                source.at[0, :, span], target.at[:, span], sems.at[kind, cut]
            )
        return pltpu.make_async_copy(source.at[0, span], target.at[span], sems.at[kind, cut])

    def arrived(kind, cut):
        if holds:
            weight_copy(kind, cut).wait()

    if holds:
        for cut in range(cuts):
            weight_copy(0, cut).start()
            weight_copy(1, cut).start()
        for cut in range(cuts):
            weight_copy(2, cut).start()
    at = 0
    for source in sources:
        rows[at : at + source.shape[0], :] = source[...]
        at += source.shape[0]
    gate_proj, up_proj = None, None
    for cut in range(cuts):
        span = slice(cut * depth, (cut + 1) * depth)
        arrived(0, cut)
        arrived(1, cut)
        gate_part = jnp.dot(rows[:, span], gate_weight[span], preferred_element_type=F32)
        up_part = jnp.dot(rows[:, span], up_weight[span], preferred_element_type=F32)
        gate_proj = gate_part if cut == 0 else gate_proj + gate_part
        up_proj = up_part if cut == 0 else up_proj + up_part
    inner_act = (gate_proj / (1.0 + jnp.exp(-gate_proj)) * up_proj).astype(BF16)
    for cut in range(cuts):
        arrived(2, cut)
        for part in range(2):
            columns = slice(cut * depth + part * width, cut * depth + (part + 1) * width)
            term = jnp.dot(inner_act, down_weight[:, columns], preferred_element_type=F32)
            store_rows(results, columns, term)


def experts_call(blocks, weights, holds, name):
    vmem = pl.BlockSpec(memory_space=pltpu.VMEM)
    anywhere = pl.BlockSpec(memory_space=pltpu.HBM)
    row_count = sum(block.shape[0] for block in blocks)
    out_shape = [jax.ShapeDtypeStruct(block.shape, BF16) for block in blocks]
    scratch = [pltpu.VMEM((row_count, blocks[0].shape[1]), BF16)]
    if holds:
        out_shape += [jax.ShapeDtypeStruct(weight.shape[1:], BF16) for weight in weights]
        scratch.append(pltpu.SemaphoreType.DMA((3, 4)))
    found = pl.pallas_call(
        functools.partial(experts_kernel, len(blocks), holds),
        out_shape=tuple(out_shape),
        in_specs=[vmem] * len(blocks) + [anywhere if holds else vmem] * 3,
        out_specs=tuple([vmem] * len(out_shape)),
        scratch_shapes=scratch,
        compiler_params=pltpu.CompilerParams(vmem_limit_bytes=VMEM_LIMIT),
        cost_estimate=pl.CostEstimate(
            flops=15 * 10**8, bytes_accessed=15 * 10**6, transcendentals=32768
        ),
        name=name,
    )(*blocks, *weights)
    return found[: len(blocks)], found[len(blocks) :]


def gather_rows(own):
    side = over_ctx(own, ACROSS)
    ahead = over_ctx(own, AHEAD)
    back = over_ctx(own, BACK)
    far = over_ctx(ahead, AHEAD)
    side_now, _ = lax.optimization_barrier((side, ahead))
    side_ahead = over_ctx(side_now, AHEAD)
    side_back = over_ctx(side_now, BACK)
    side_far = over_ctx(far, ACROSS)
    return (ahead, back, side), (far, side_ahead, side_back, side_far)


def added(*terms):
    total = terms[0].astype(F32)
    for term in terms[1:]:
        total = total + term.astype(F32)
    return total.astype(BF16)


def reduce_rows(own, near, far):
    ahead, back, side = near
    far, side_ahead, side_back, side_far = far
    side_far_in = over_ctx(side_far, ACROSS)
    side_ahead_in = over_ctx(side_ahead, BACK)
    side_back_in = over_ctx(side_back, AHEAD)
    far_in = over_ctx(added(far, side_far_in), BACK)
    side_in = over_ctx(added(side, side_ahead_in, side_back_in), ACROSS)
    back_in = over_ctx(back, AHEAD)
    ahead_in = over_ctx(added(ahead, far_in), BACK)
    return added(own, back_in, side_in, ahead_in)


def on_device(
    queries,
    prior_codes,
    fresh_codes,
    prior_powers,
    fresh_powers,
    block_mask,
    value_up,
    output_weight,
    residual,
    norm_gain,
    router,
    route_ids,
    gate_weight,
    up_weight,
    down_weight,
):
    ctx_index = lax.axis_index("ctx")
    core = lax.axis_index("exp") % CORES
    rows_block, head_count, key_width = queries.shape
    prior_blocks = prior_powers.shape[0]
    scales = power_two(jnp.concatenate([prior_powers, fresh_powers], axis=0))
    blocks_here = jnp.concatenate(
        [jnp.transpose(prior_codes), jnp.transpose(fresh_codes)], axis=1
    ).reshape(key_width, prior_blocks + 1, rows_block)
    blocks_here = jnp.transpose(blocks_here, (1, 0, 2)).astype(F32)
    blocks_here = (blocks_here * scales[:, None, None]).astype(BF16)
    near, far_blocks = gather_codes(blocks_here, core)
    live = block_flags(block_mask, ctx_index, core, prior_blocks)
    groups = rows_block // 16
    split = queries.reshape(groups, 2, 8, head_count, key_width)
    first = jnp.where(core == 0, split[:, 0], split[:, 1])
    second = jnp.where(core == 0, split[:, 1], split[:, 0])
    ordered = jnp.stack([first, second], axis=0)
    ordered = jnp.transpose(ordered, (3, 0, 1, 2, 4)).reshape(head_count * rows_block, key_width)

    state = near_call(live, ordered, near, value_up)
    *state, done = state
    far = far_blocks(done)
    keep, send = far_call(live, ordered, far, state, value_up, output_weight)
    expert_count = router.shape[1]
    token_count, route_count = route_ids.shape
    capacity = token_count * route_count * 2 // expert_count
    route_hits = route_ids[:, :, None] == jnp.arange(expert_count)[None, None, :]
    flat_hits = route_hits.reshape(token_count * route_count, expert_count).astype(jnp.int32)
    before = jnp.cumsum(flat_hits, axis=0) - flat_hits
    slot_index = jnp.sum(before * flat_hits, axis=1)
    target = route_ids.reshape(-1) * capacity + slot_index
    placing = (target[None, :] == jnp.arange(expert_count * capacity)[:, None]).astype(BF16)
    placing_back = jnp.transpose(placing)
    gain = norm_gain.astype(F32)
    keep, send, placing, placing_back, route_ids, gain = lax.optimization_barrier(
        (keep, send, placing, placing_back, route_ids, gain)
    )
    paired = added(keep, core_swap(send))
    model_width = residual.shape[1]
    pieces = lax.all_to_all(
        paired.reshape(groups, 8, model_width),
        "exp",
        split_axis=0,
        concat_axis=0,
        tiled=True,
        axis_index_groups=SAME_CORE,
    )
    attention = jnp.sum(pieces.astype(F32), axis=0)
    hidden = (residual.astype(F32) + attention).astype(BF16)
    hidden_wide = hidden.astype(F32)
    normed = (
        hidden_wide
        * lax.rsqrt(jnp.mean(hidden_wide * hidden_wide, axis=1, keepdims=True) + 1e-06)
        * gain
    ).astype(BF16)
    affinity = jax.nn.sigmoid(jnp.dot(normed, router, preferred_element_type=F32))
    route_hits = route_ids[:, :, None] == jnp.arange(expert_count)[None, None, :]
    chosen = jnp.sum(jnp.where(route_hits, affinity[:, None, :], 0.0), axis=2)
    gate_values = 2.5 * chosen / jnp.sum(chosen, axis=1, keepdims=True)
    repeated = jnp.repeat(normed, route_count, axis=0)
    buffer = jnp.dot(placing, repeated, preferred_element_type=F32).astype(BF16)
    sectioned = lax.all_to_all(
        buffer.reshape(expert_count, capacity, model_width),
        "exp",
        split_axis=0,
        concat_axis=0,
        tiled=True,
    )
    own_rows = sectioned.reshape(expert_count * capacity, model_width)
    near_rows, far_rows = gather_rows(own_rows)
    near_terms, weights = experts_call(
        (own_rows,) + near_rows, (gate_weight, up_weight, down_weight), True, "experts_near"
    )
    far_terms, _ = experts_call(far_rows, weights, False, "experts_far")
    summed = reduce_rows(near_terms[0], near_terms[1:], far_terms)
    summed, gate_values, hidden = lax.optimization_barrier((summed, gate_values, hidden))
    returned = lax.all_to_all(
        summed.reshape(expert_count, capacity, model_width),
        "exp",
        split_axis=0,
        concat_axis=0,
        tiled=True,
    ).reshape(expert_count * capacity, model_width)
    gathered_back = jnp.dot(
        placing_back, returned, preferred_element_type=F32
    ).reshape(token_count, route_count, model_width)
    expert_mix = jnp.sum(gate_values[:, :, None] * gathered_back, axis=1)
    return (hidden.astype(F32) + expert_mix).astype(BF16)


def solution(mesh):
    in_specs = (
        P("ctx", "exp", None),
        P("ctx", None),
        P("ctx", None),
        P("ctx"),
        P("ctx"),
        P(),
        P("exp", None, None),
        P("exp", None),
        P(("ctx", "exp"), None),
        P(),
        P(),
        P(("ctx", "exp"), None),
        P("exp", None, "ctx"),
        P("exp", None, "ctx"),
        P("exp", "ctx", None),
    )
    out_specs = P(("ctx", "exp"), None)
    return jax.shard_map(
        on_device, mesh=mesh, in_specs=in_specs, out_specs=out_specs, check_vma=False
    )
```

```python
import functools

import jax
import jax.numpy as jnp
from jax import lax
from jax.experimental import pallas as pl
from jax.experimental.pallas import tpu as pltpu
from jax.sharding import PartitionSpec as P

ROPE = 64
NOPE = 128
Y_HI, Z, Y_LO, X, CORES = 2, 4, 2, 4, 2
STEP_BLOCKS = 4
VMEM_LIMIT = 36 * 2**20
HEADS_HERE = 4
F32 = jnp.float32
BF16 = jnp.bfloat16


def ctx_pairs(move):
    pairs = []
    for y in range(Y_HI):
        for z in range(Z):
            for i in range(Y_LO * X * CORES):
                to_y, to_z = move(y, z, 1 - 2 * (i % CORES))
                pairs.append(
                    (
                        (y * Z + z) * Y_LO * X * CORES + i,
                        (to_y * Z + to_z) * Y_LO * X * CORES + i,
                    )
                )
    return pairs


AHEAD = ctx_pairs(lambda y, z, way: (y, (z + way) % Z))
BACK = ctx_pairs(lambda y, z, way: (y, (z - way) % Z))
ACROSS = ctx_pairs(lambda y, z, way: (1 - y, z))
CORE_SWAP = [(i, i ^ 1) for i in range(Y_LO * X * CORES)]
SAME_CORE = [[2 * i + core for i in range(Y_LO * X)] for core in range(CORES)]


def over_ctx(value, pairs):
    return lax.ppermute(value, ("ctx", "exp"), pairs)


def core_swap(value):
    return lax.ppermute(value, "exp", CORE_SWAP)


def power_two(powers):
    return jnp.where(powers < 0, 0.5, jnp.where(powers > 0, 2.0, 1.0)).astype(jnp.float32)


def in_hbm(value):
    return pltpu.with_memory_space_constraint(value, pltpu.HBM)


def attend(mask, queries, steps, diagonal, scores, top, total, mixture):
    rows = queries.shape[0]
    latent_width = mixture.shape[1]
    block = top.shape[1]
    factor = 1.4426950408889634 / (NOPE + ROPE) ** 0.5
    top[...] = jnp.full_like(top, -1e30)
    total[...] = jnp.zeros_like(total)
    mixture[...] = jnp.zeros_like(mixture)

    def keys_of(step, height):
        return jnp.concatenate([part[i, :height] for part, i, _ in step], axis=1)

    def lane_fold(value, fold):
        folded = value[:, :block]
        for i in range(1, STEP_BLOCKS):
            folded = fold(folded, value[:, i * block : (i + 1) * block])
        return folded

    ctx_index = lax.axis_index("ctx")
    core = lax.axis_index("exp") % CORES
    owners = mask.shape[0]
    prior_blocks = mask.shape[1] // owners - 1

    def flag(place):
        dy, dz, number = place
        owner = (ctx_index // Z + dy) % Y_HI * Z + (ctx_index % Z + dz + Z) % Z
        prior = owner * prior_blocks + jnp.minimum(number, prior_blocks - 1)
        fresh = owners * prior_blocks + owner
        return mask[ctx_index, jnp.where(number < prior_blocks, prior, fresh)]

    def flags_of(number):
        return [flag(place) for _, _, place in steps[number]]

    def score(step, number):
        flags = flags_of(number)

        @pl.when(sum(flags) > 0)
        def _():
            found = jnp.dot(
                queries[...], keys_of(step, queries.shape[1]), preferred_element_type=F32
            )
            column = lax.broadcasted_iota(jnp.int32, (1, STEP_BLOCKS * block), 1) // block
            shown = jnp.zeros(column.shape, jnp.int32)
            for i, flag in enumerate(flags):
                shown = jnp.where(column == i, flag, shown)
            found = jnp.where(shown > 0, found, -1e30)
            if diagonal and number == 0:
                last = (STEP_BLOCKS - 1) * block
                seen = jnp.where(causal(), found[:, last:], -1e30)
                found = jnp.concatenate([found[:, :last], seen], axis=1)
            scores[number] = found
            top[...] = jnp.maximum(top[...], lane_fold(found, jnp.maximum))

    def causal():
        tokens = rows // HEADS_HERE
        row = lax.broadcasted_iota(jnp.int32, (rows, 1), 0) % tokens
        relative = row // (tokens // 2)
        within = row % (tokens // 2)
        side = jnp.where(relative == 0, core, 1 - core)
        token = within // 8 * 16 + side * 8 + within % 8
        return lax.broadcasted_iota(jnp.int32, (1, block), 1) <= token

    for number, step in enumerate(steps):
        score(step, number)
    row_top = jnp.max(top[...], axis=1, keepdims=True)

    def mix(step, number):
        @pl.when(sum(flags_of(number)) > 0)
        def _():
            weights = jnp.exp2((scores[number] - row_top) * factor)
            total[...] += lane_fold(weights, jnp.add)
            mixture[...] += lax.dot_general(
                weights.astype(BF16),
                keys_of(step, latent_width),
                (((1,), (1,)), ((), ())),
                preferred_element_type=F32,
            )

    for number, step in enumerate(steps):
        mix(step, number)
    return row_top


def whole(part, dy, dz):
    return [(part, i, (dy, dz, i)) for i in range(STEP_BLOCKS)]


def halves(part, other, dy, dz, first):
    half = STEP_BLOCKS // 2
    return [
        (array, i, (dy, dz, start + i))
        for array, start in ((part, first), (other, half - first))
        for i in range(half)
    ]


def near_kernel(
    mask, queries, own, beside, beside_other, side, side_other, weight_hbm,
    top, total, mixture, weight, done, scores, weight_sem,
):
    copy = pltpu.make_async_copy(weight_hbm, weight, weight_sem)
    copy.start()
    core = lax.axis_index("exp") % CORES
    way = 1 - 2 * core
    first = core * (STEP_BLOCKS // 2)
    steps = [
        whole(own, 0, 0),
        whole(beside, 0, -way),
        whole(beside_other, 0, way),
        halves(side, side_other, 1, 0, first),
    ]
    row_top = attend(mask, queries, steps, True, scores, top, total, mixture)
    top[...] = jnp.broadcast_to(row_top, top.shape)
    done[...] = jnp.ones_like(done)
    copy.wait()


def far_kernel(
    mask, queries, beside, beside_other, far, far_other, side_far, side_far_other,
    near_top, near_total, near_mixture, weight, value_up,
    out_keep, out_send, scores, top, total, mixture,
):
    heads = value_up.shape[0]
    tokens = queries.shape[0] // heads
    factor = 1.4426950408889634 / (NOPE + ROPE) ** 0.5
    core = lax.axis_index("exp") % CORES
    way = 1 - 2 * core
    half = STEP_BLOCKS // 2
    first = core * half

    def sent(part, dz, first):
        low = [(part, i, (1, dz, first + i)) for i in range(half)]
        return low + [(part, half + i, (1, dz, half - first + i)) for i in range(half)]

    steps = [
        sent(beside, -way, first),
        sent(beside_other, way, half - first),
        halves(far, far_other, 0, 2, first),
        halves(side_far, side_far_other, 1, 2, first),
    ]
    far_top = attend(mask, queries, steps, False, scores, top, total, mixture)
    near_row_top = near_top[:, :1]
    both_top = jnp.maximum(near_row_top, far_top)
    near_scale = jnp.exp2((near_row_top - both_top) * factor)
    far_scale = jnp.exp2((far_top - both_top) * factor)
    row_total = jnp.sum(near_total[...] * near_scale + total[...] * far_scale, axis=1, keepdims=True)
    near_scale = near_scale / row_total
    far_scale = far_scale / row_total
    per_head = []
    for head in range(heads):
        span = slice(head * tokens, (head + 1) * tokens)
        attended = near_mixture[span] * near_scale[span] + mixture[span] * far_scale[span]
        per_head.append(
            jnp.dot(
                attended.astype(BF16), value_up[head], preferred_element_type=F32
            ).astype(BF16)
        )
    flat_heads = jnp.concatenate(per_head, axis=1)
    out_width = 1024
    half = tokens // 2

    for step in range(weight.shape[1] // out_width):
        columns = slice(step * out_width, (step + 1) * out_width)
        term = jnp.dot(flat_heads, weight[:, columns], preferred_element_type=F32)
        out_keep[:, columns] = term[:half].astype(BF16)
        out_send[:, columns] = term[half:].astype(BF16)


def score_scratch(blocks, rows, block):
    return pltpu.VMEM((blocks // STEP_BLOCKS, rows, STEP_BLOCKS * block), F32)


def near_call(mask, queries, near, value_up, output_weight):
    rows, block = queries.shape[0], near[0].shape[2]
    vmem = pl.BlockSpec(memory_space=pltpu.VMEM)
    lanes = jax.ShapeDtypeStruct((rows, block), F32)
    return pl.pallas_call(
        near_kernel,
        out_shape=(
            lanes,
            lanes,
            jax.ShapeDtypeStruct((rows, value_up.shape[1]), F32),
            pltpu.VMEM(output_weight.shape, BF16),
            jax.ShapeDtypeStruct((8, block), F32),
        ),
        in_specs=[pl.BlockSpec(memory_space=pltpu.SMEM)]
        + [vmem] * (1 + len(near))
        + [pl.BlockSpec(memory_space=pltpu.HBM)],
        out_specs=(vmem,) * 5,
        scratch_shapes=[
            score_scratch(sum(part.shape[0] for part in near), rows, block),
            pltpu.SemaphoreType.DMA,
        ],
        compiler_params=pltpu.CompilerParams(vmem_limit_bytes=32 * 2**20),
        cost_estimate=pl.CostEstimate(
            flops=3 * 10**9, bytes_accessed=12 * 10**6, transcendentals=10**6
        ),
        name="attention_near",
    )(mask, queries, *near, in_hbm(output_weight))


def far_call(mask, queries, far, state, value_up):
    rows, block = queries.shape[0], far[0].shape[2]
    tokens = rows // value_up.shape[0]
    vmem = pl.BlockSpec(memory_space=pltpu.VMEM)
    out = jax.ShapeDtypeStruct((tokens // 2, state[3].shape[1]), BF16)
    return pl.pallas_call(
        far_kernel,
        out_shape=(out, out),
        in_specs=[pl.BlockSpec(memory_space=pltpu.SMEM)]
        + [vmem] * (2 + len(far) + len(state)),
        out_specs=(vmem, vmem),
        scratch_shapes=[
            score_scratch(sum(part.shape[0] for part in far), rows, block),
            pltpu.VMEM((rows, block), F32),
            pltpu.VMEM((rows, block), F32),
            pltpu.VMEM((rows, value_up.shape[1]), F32),
        ],
        compiler_params=pltpu.CompilerParams(vmem_limit_bytes=32 * 2**20),
        cost_estimate=pl.CostEstimate(
            flops=4 * 10**9, bytes_accessed=14 * 10**6, transcendentals=10**6
        ),
        name="attention_far",
    )(mask, queries, *far, *state, value_up)


def own_half(blocks, core):
    half_blocks = blocks.shape[0] // 2
    return lax.dynamic_slice_in_dim(blocks, core * half_blocks, half_blocks, 0)


def after(value, event):
    one = event[(0,) * event.ndim].astype(F32) * 0.0 + 1.0
    tile = value[(slice(0, 1),) * (value.ndim - 2) + (slice(0, 16), slice(0, 128))]
    tile = (tile.astype(F32) * one).astype(value.dtype)
    return lax.dynamic_update_slice(value, tile, (0,) * value.ndim)


def gather_codes(blocks, core):
    blocks = lax.optimization_barrier(blocks)
    beside = over_ctx(blocks, AHEAD)
    side = over_ctx(own_half(blocks, core), ACROSS)
    beside_half = own_half(beside, core)
    far = over_ctx(beside_half, AHEAD)
    side_other, _ = lax.optimization_barrier((core_swap(side), beside_half))
    side_beside = over_ctx(jnp.concatenate([side, side_other], axis=0), AHEAD)
    side_far = over_ctx(far, ACROSS)
    near = (blocks, beside, core_swap(beside), side, side_other)

    def far_blocks(done):
        held = after(side_far, done)
        swapped = [core_swap(part) for part in (side_beside, far, held)]
        return (side_beside, swapped[0], far, swapped[1], held, swapped[2])

    return near, far_blocks


def store_rows(results, columns, term):
    at = 0
    for result in results:
        result[:, columns] = term[at : at + result.shape[0]].astype(BF16)
        at += result.shape[0]


def experts_kernel(count, holds, *refs):
    sources, weights_in = refs[:count], refs[count : count + 3]
    results = refs[count + 3 : 2 * count + 3]
    if holds:
        gate_weight, up_weight, down_weight, rows, sems = refs[2 * count + 3 :]
    else:
        gate_weight, up_weight, down_weight = weights_in
        (rows,) = refs[2 * count + 3 :]
    cuts = 4
    depth = rows.shape[1] // cuts
    width = depth // 2

    def weight_copy(kind, cut):
        span = slice(cut * depth, (cut + 1) * depth)
        source, target = weights_in[kind], (gate_weight, up_weight, down_weight)[kind]
        if kind == 2:
            return pltpu.make_async_copy(
                source.at[0, :, span], target.at[:, span], sems.at[kind, cut]
            )
        return pltpu.make_async_copy(source.at[0, span], target.at[span], sems.at[kind, cut])

    def arrived(kind, cut):
        if holds:
            weight_copy(kind, cut).wait()

    if holds:
        for cut in range(cuts):
            weight_copy(0, cut).start()
            weight_copy(1, cut).start()
        for cut in range(cuts):
            weight_copy(2, cut).start()
    at = 0
    for source in sources:
        rows[at : at + source.shape[0], :] = source[...]
        at += source.shape[0]
    gate_proj, up_proj = None, None
    for cut in range(cuts):
        span = slice(cut * depth, (cut + 1) * depth)
        arrived(0, cut)
        arrived(1, cut)
        gate_part = jnp.dot(rows[:, span], gate_weight[span], preferred_element_type=F32)
        up_part = jnp.dot(rows[:, span], up_weight[span], preferred_element_type=F32)
        gate_proj = gate_part if cut == 0 else gate_proj + gate_part
        up_proj = up_part if cut == 0 else up_proj + up_part
    inner_act = (gate_proj / (1.0 + jnp.exp(-gate_proj)) * up_proj).astype(BF16)
    for cut in range(cuts):
        arrived(2, cut)
        for part in range(2):
            columns = slice(cut * depth + part * width, cut * depth + (part + 1) * width)
            term = jnp.dot(inner_act, down_weight[:, columns], preferred_element_type=F32)
            store_rows(results, columns, term)


def experts_call(blocks, weights, holds, name):
    vmem = pl.BlockSpec(memory_space=pltpu.VMEM)
    anywhere = pl.BlockSpec(memory_space=pltpu.HBM)
    row_count = sum(block.shape[0] for block in blocks)
    out_shape = [jax.ShapeDtypeStruct(block.shape, BF16) for block in blocks]
    scratch = [pltpu.VMEM((row_count, blocks[0].shape[1]), BF16)]
    if holds:
        out_shape += [pltpu.VMEM(weight.shape[1:], BF16) for weight in weights]
        weights = [in_hbm(weight) for weight in weights]
        scratch.append(pltpu.SemaphoreType.DMA((3, 4)))
    found = pl.pallas_call(
        functools.partial(experts_kernel, len(blocks), holds),
        out_shape=tuple(out_shape),
        in_specs=[vmem] * len(blocks) + [anywhere if holds else vmem] * 3,
        out_specs=tuple([vmem] * len(out_shape)),
        scratch_shapes=scratch,
        compiler_params=pltpu.CompilerParams(vmem_limit_bytes=VMEM_LIMIT),
        cost_estimate=pl.CostEstimate(
            flops=15 * 10**8, bytes_accessed=15 * 10**6, transcendentals=32768
        ),
        name=name,
    )(*blocks, *weights)
    return found[: len(blocks)], found[len(blocks) :]


def gather_rows(own):
    side = over_ctx(own, ACROSS)
    ahead = over_ctx(own, AHEAD)
    back = over_ctx(own, BACK)
    far = over_ctx(ahead, AHEAD)
    side_now, _ = lax.optimization_barrier((side, ahead))
    side_ahead = over_ctx(side_now, AHEAD)
    side_back = over_ctx(side_now, BACK)
    side_far = over_ctx(far, ACROSS)
    return (ahead, back, side), (far, side_ahead, side_back, side_far)


def added(*terms):
    total = terms[0].astype(F32)
    for term in terms[1:]:
        total = total + term.astype(F32)
    return total.astype(BF16)


def reduce_rows(own, near, far):
    ahead, back, side = near
    far, side_ahead, side_back, side_far = far
    side_far_in = over_ctx(side_far, ACROSS)
    side_ahead_in = over_ctx(side_ahead, BACK)
    side_back_in = over_ctx(side_back, AHEAD)
    far_in = over_ctx(added(far, side_far_in), BACK)
    side_in = over_ctx(added(side, side_ahead_in, side_back_in), ACROSS)
    back_in = over_ctx(back, AHEAD)
    ahead_in = over_ctx(added(ahead, far_in), BACK)
    return added(own, back_in, side_in, ahead_in)


def on_device(
    queries,
    prior_codes,
    fresh_codes,
    prior_powers,
    fresh_powers,
    block_mask,
    value_up,
    output_weight,
    residual,
    norm_gain,
    router,
    route_ids,
    gate_weight,
    up_weight,
    down_weight,
):
    core = lax.axis_index("exp") % CORES
    rows_block, head_count, key_width = queries.shape
    prior_blocks = prior_powers.shape[0]
    scales = power_two(jnp.concatenate([prior_powers, fresh_powers], axis=0))
    blocks_here = jnp.concatenate(
        [jnp.transpose(prior_codes), jnp.transpose(fresh_codes)], axis=1
    ).reshape(key_width, prior_blocks + 1, rows_block)
    blocks_here = jnp.transpose(blocks_here, (1, 0, 2)).astype(F32)
    blocks_here = (blocks_here * scales[:, None, None]).astype(BF16)
    near, far_blocks = gather_codes(blocks_here, core)
    groups = rows_block // 16
    split = queries.reshape(groups, 2, 8, head_count, key_width)
    first = jnp.where(core == 0, split[:, 0], split[:, 1])
    second = jnp.where(core == 0, split[:, 1], split[:, 0])
    ordered = jnp.stack([first, second], axis=0)
    ordered = jnp.transpose(ordered, (3, 0, 1, 2, 4)).reshape(head_count * rows_block, key_width)

    state = near_call(block_mask, ordered, near, value_up, output_weight)
    *state, done = state
    far = far_blocks(done)
    keep, send = far_call(block_mask, ordered, far, state, value_up)
    expert_count = router.shape[1]
    token_count, route_count = route_ids.shape
    capacity = token_count * route_count * 2 // expert_count
    route_hits = route_ids[:, :, None] == jnp.arange(expert_count)[None, None, :]
    flat_hits = route_hits.reshape(token_count * route_count, expert_count).astype(jnp.int32)
    before = jnp.cumsum(flat_hits, axis=0) - flat_hits
    slot_index = jnp.sum(before * flat_hits, axis=1)
    target = route_ids.reshape(-1) * capacity + slot_index
    placing = (target[None, :] == jnp.arange(expert_count * capacity)[:, None]).astype(BF16)
    placing_back = jnp.transpose(placing)
    gain = norm_gain.astype(F32)
    keep, send, placing, placing_back, route_ids, gain = lax.optimization_barrier(
        (keep, send, placing, placing_back, route_ids, gain)
    )
    paired = added(keep, core_swap(send))
    model_width = residual.shape[1]
    pieces = lax.all_to_all(
        paired.reshape(groups, 8, model_width),
        "exp",
        split_axis=0,
        concat_axis=0,
        tiled=True,
        axis_index_groups=SAME_CORE,
    )
    attention = jnp.sum(pieces.astype(F32), axis=0)
    hidden = (residual.astype(F32) + attention).astype(BF16)
    hidden_wide = hidden.astype(F32)
    normed = (
        hidden_wide
        * lax.rsqrt(jnp.mean(hidden_wide * hidden_wide, axis=1, keepdims=True) + 1e-06)
        * gain
    ).astype(BF16)
    affinity = jax.nn.sigmoid(jnp.dot(normed, router, preferred_element_type=F32))
    route_hits = route_ids[:, :, None] == jnp.arange(expert_count)[None, None, :]
    chosen = jnp.sum(jnp.where(route_hits, affinity[:, None, :], 0.0), axis=2)
    gate_values = 2.5 * chosen / jnp.sum(chosen, axis=1, keepdims=True)
    repeated = jnp.repeat(normed, route_count, axis=0)
    buffer = jnp.dot(placing, repeated, preferred_element_type=F32).astype(BF16)
    sectioned = lax.all_to_all(
        buffer.reshape(expert_count, capacity, model_width),
        "exp",
        split_axis=0,
        concat_axis=0,
        tiled=True,
    )
    own_rows = sectioned.reshape(expert_count * capacity, model_width)
    near_rows, far_rows = gather_rows(own_rows)
    near_terms, weights = experts_call(
        (own_rows,) + near_rows, (gate_weight, up_weight, down_weight), True, "experts_near"
    )
    far_terms, _ = experts_call(far_rows, weights, False, "experts_far")
    summed = reduce_rows(near_terms[0], near_terms[1:], far_terms)
    summed, gate_values, hidden = lax.optimization_barrier((summed, gate_values, hidden))
    returned = lax.all_to_all(
        summed.reshape(expert_count, capacity, model_width),
        "exp",
        split_axis=0,
        concat_axis=0,
        tiled=True,
    ).reshape(expert_count * capacity, model_width)
    gathered_back = jnp.dot(
        placing_back, returned, preferred_element_type=F32
    ).reshape(token_count, route_count, model_width)
    expert_mix = jnp.sum(gate_values[:, :, None] * gathered_back, axis=1)
    return (hidden.astype(F32) + expert_mix).astype(BF16)


def solution(mesh):
    in_specs = (
        P("ctx", "exp", None),
        P("ctx", None),
        P("ctx", None),
        P("ctx"),
        P("ctx"),
        P(),
        P("exp", None, None),
        P("exp", None),
        P(("ctx", "exp"), None),
        P(),
        P(),
        P(("ctx", "exp"), None),
        P("exp", None, "ctx"),
        P("exp", None, "ctx"),
        P("exp", "ctx", None),
    )
    out_specs = P(("ctx", "exp"), None)
    return jax.shard_map(
        on_device, mesh=mesh, in_specs=in_specs, out_specs=out_specs, check_vma=False
    )
```

```python
import functools

import jax
import jax.numpy as jnp
from jax import lax
from jax.experimental import pallas as pl
from jax.experimental.pallas import tpu as pltpu
from jax.sharding import PartitionSpec as P

ROPE = 64
NOPE = 128
Y_HI, Z, Y_LO, X, CORES = 2, 4, 2, 4, 2
STEP_BLOCKS = 4
VMEM_LIMIT = 36 * 2**20
HEADS_HERE = 4
F32 = jnp.float32
BF16 = jnp.bfloat16


def ctx_pairs(move):
    pairs = []
    for y in range(Y_HI):
        for z in range(Z):
            for i in range(Y_LO * X * CORES):
                to_y, to_z = move(y, z, 1 - 2 * (i % CORES))
                pairs.append(
                    (
                        (y * Z + z) * Y_LO * X * CORES + i,
                        (to_y * Z + to_z) * Y_LO * X * CORES + i,
                    )
                )
    return pairs


AHEAD = ctx_pairs(lambda y, z, way: (y, (z + way) % Z))
BACK = ctx_pairs(lambda y, z, way: (y, (z - way) % Z))
ACROSS = ctx_pairs(lambda y, z, way: (1 - y, z))
CORE_SWAP = [(i, i ^ 1) for i in range(Y_LO * X * CORES)]
SAME_CORE = [[2 * i + core for i in range(Y_LO * X)] for core in range(CORES)]


def over_ctx(value, pairs):
    return lax.ppermute(value, ("ctx", "exp"), pairs)


def core_swap(value):
    return lax.ppermute(value, "exp", CORE_SWAP)


def power_two(powers):
    return jnp.where(powers < 0, 0.5, jnp.where(powers > 0, 2.0, 1.0)).astype(jnp.float32)


def in_hbm(value):
    return pltpu.with_memory_space_constraint(value, pltpu.HBM)


def attend(mask, queries, steps, diagonal, scores, top, total, mixture):
    rows = queries.shape[0]
    latent_width = mixture.shape[1]
    block = top.shape[1]
    factor = 1.4426950408889634 / (NOPE + ROPE) ** 0.5
    top[...] = jnp.full_like(top, -1e30)
    total[...] = jnp.zeros_like(total)
    mixture[...] = jnp.zeros_like(mixture)

    def keys_of(step, height):
        return jnp.concatenate([part[i, :height] for part, i, _ in step], axis=1)

    def lane_fold(value, fold):
        folded = value[:, :block]
        for i in range(1, STEP_BLOCKS):
            folded = fold(folded, value[:, i * block : (i + 1) * block])
        return folded

    ctx_index = lax.axis_index("ctx")
    core = lax.axis_index("exp") % CORES
    owners = mask.shape[0]
    prior_blocks = mask.shape[1] // owners - 1

    def flag(place):
        dy, dz, number = place
        owner = (ctx_index // Z + dy) % Y_HI * Z + (ctx_index % Z + dz + Z) % Z
        prior = owner * prior_blocks + jnp.minimum(number, prior_blocks - 1)
        fresh = owners * prior_blocks + owner
        return mask[ctx_index, jnp.where(number < prior_blocks, prior, fresh)]

    def flags_of(number):
        return [flag(place) for _, _, place in steps[number]]

    all_flags = [flags_of(number) for number in range(len(steps))]
    live = [(sum(flags) > 0).astype(jnp.int32) for flags in all_flags]
    straight = sum(live) >= len(steps) - 1

    def score(step, number):
        found = jnp.dot(
            queries[...], keys_of(step, queries.shape[1]), preferred_element_type=F32
        )
        column = lax.broadcasted_iota(jnp.int32, (1, STEP_BLOCKS * block), 1) // block
        shown = jnp.zeros(column.shape, jnp.int32)
        for i, flag in enumerate(all_flags[number]):
            shown = jnp.where(column == i, flag, shown)
        found = jnp.where(shown > 0, found, -1e30)
        if diagonal and number == 0:
            last = (STEP_BLOCKS - 1) * block
            seen = jnp.where(causal(), found[:, last:], -1e30)
            found = jnp.concatenate([found[:, :last], seen], axis=1)
        scores[number] = found
        top[...] = jnp.maximum(top[...], lane_fold(found, jnp.maximum))

    def causal():
        tokens = rows // HEADS_HERE
        row = lax.broadcasted_iota(jnp.int32, (rows, 1), 0) % tokens
        relative = row // (tokens // 2)
        within = row % (tokens // 2)
        side = jnp.where(relative == 0, core, 1 - core)
        token = within // 8 * 16 + side * 8 + within % 8
        return lax.broadcasted_iota(jnp.int32, (1, block), 1) <= token

    def mix(row_top, step, number):
        weights = jnp.exp2((scores[number] - row_top) * factor)
        total[...] += lane_fold(weights, jnp.add)
        mixture[...] += lax.dot_general(
            weights.astype(BF16),
            keys_of(step, latent_width),
            (((1,), (1,)), ((), ())),
            preferred_element_type=F32,
        )

    def all_steps(branches):
        def each_step(body):
            for number, step in enumerate(steps):
                if branches:
                    pl.when(live[number] > 0)(functools.partial(body, step, number))
                else:
                    body(step, number)

        each_step(score)
        row_top = jnp.max(top[...], axis=1, keepdims=True)
        each_step(functools.partial(mix, row_top))
        top[...] = jnp.broadcast_to(row_top, top.shape)

    pl.when(straight)(functools.partial(all_steps, False))
    pl.when(jnp.logical_not(straight))(functools.partial(all_steps, True))


def whole(part, dy, dz):
    return [(part, i, (dy, dz, i)) for i in range(STEP_BLOCKS)]


def halves(part, other, dy, dz, first):
    half = STEP_BLOCKS // 2
    return [
        (array, i, (dy, dz, start + i))
        for array, start in ((part, first), (other, half - first))
        for i in range(half)
    ]


def near_kernel(
    mask, queries, own, beside, beside_other, side, side_other, weight_hbm,
    top, total, mixture, weight, done, scores, weight_sem,
):
    copy = pltpu.make_async_copy(weight_hbm, weight, weight_sem)
    copy.start()
    core = lax.axis_index("exp") % CORES
    way = 1 - 2 * core
    first = core * (STEP_BLOCKS // 2)
    steps = [
        whole(own, 0, 0),
        whole(beside, 0, -way),
        whole(beside_other, 0, way),
        halves(side, side_other, 1, 0, first),
    ]
    attend(mask, queries, steps, True, scores, top, total, mixture)
    done[...] = jnp.ones_like(done)
    copy.wait()


def far_kernel(
    mask, queries, beside, beside_other, far, far_other, side_far, side_far_other,
    near_top, near_total, near_mixture, weight, value_up,
    out_keep, out_send, scores, top, total, mixture,
):
    heads = value_up.shape[0]
    tokens = queries.shape[0] // heads
    factor = 1.4426950408889634 / (NOPE + ROPE) ** 0.5
    core = lax.axis_index("exp") % CORES
    way = 1 - 2 * core
    half = STEP_BLOCKS // 2
    first = core * half

    def sent(part, dz, first):
        low = [(part, i, (1, dz, first + i)) for i in range(half)]
        return low + [(part, half + i, (1, dz, half - first + i)) for i in range(half)]

    steps = [
        sent(beside, -way, first),
        sent(beside_other, way, half - first),
        halves(far, far_other, 0, 2, first),
        halves(side_far, side_far_other, 1, 2, first),
    ]
    attend(mask, queries, steps, False, scores, top, total, mixture)
    far_top = top[:, :1]
    near_row_top = near_top[:, :1]
    both_top = jnp.maximum(near_row_top, far_top)
    near_scale = jnp.exp2((near_row_top - both_top) * factor)
    far_scale = jnp.exp2((far_top - both_top) * factor)
    row_total = jnp.sum(near_total[...] * near_scale + total[...] * far_scale, axis=1, keepdims=True)
    near_scale = near_scale / row_total
    far_scale = far_scale / row_total
    per_head = []
    for head in range(heads):
        span = slice(head * tokens, (head + 1) * tokens)
        attended = near_mixture[span] * near_scale[span] + mixture[span] * far_scale[span]
        per_head.append(
            jnp.dot(
                attended.astype(BF16), value_up[head], preferred_element_type=F32
            ).astype(BF16)
        )
    flat_heads = jnp.concatenate(per_head, axis=1)
    out_width = 1024
    half = tokens // 2

    for step in range(weight.shape[1] // out_width):
        columns = slice(step * out_width, (step + 1) * out_width)
        term = jnp.dot(flat_heads, weight[:, columns], preferred_element_type=F32)
        out_keep[:, columns] = term[:half].astype(BF16)
        out_send[:, columns] = term[half:].astype(BF16)


def score_scratch(blocks, rows, block):
    return pltpu.VMEM((blocks // STEP_BLOCKS, rows, STEP_BLOCKS * block), F32)


def near_call(mask, queries, near, value_up, output_weight):
    rows, block = queries.shape[0], near[0].shape[2]
    vmem = pl.BlockSpec(memory_space=pltpu.VMEM)
    lanes = jax.ShapeDtypeStruct((rows, block), F32)
    return pl.pallas_call(
        near_kernel,
        out_shape=(
            lanes,
            lanes,
            jax.ShapeDtypeStruct((rows, value_up.shape[1]), F32),
            pltpu.VMEM(output_weight.shape, BF16),
            jax.ShapeDtypeStruct((8, block), F32),
        ),
        in_specs=[pl.BlockSpec(memory_space=pltpu.SMEM)]
        + [vmem] * (1 + len(near))
        + [pl.BlockSpec(memory_space=pltpu.HBM)],
        out_specs=(vmem,) * 5,
        scratch_shapes=[
            score_scratch(sum(part.shape[0] for part in near), rows, block),
            pltpu.SemaphoreType.DMA,
        ],
        compiler_params=pltpu.CompilerParams(vmem_limit_bytes=32 * 2**20),
        cost_estimate=pl.CostEstimate(
            flops=3 * 10**9, bytes_accessed=12 * 10**6, transcendentals=10**6
        ),
        name="attention_near",
    )(mask, queries, *near, in_hbm(output_weight))


def far_call(mask, queries, far, state, value_up):
    rows, block = queries.shape[0], far[0].shape[2]
    tokens = rows // value_up.shape[0]
    vmem = pl.BlockSpec(memory_space=pltpu.VMEM)
    out = jax.ShapeDtypeStruct((tokens // 2, state[3].shape[1]), BF16)
    return pl.pallas_call(
        far_kernel,
        out_shape=(out, out),
        in_specs=[pl.BlockSpec(memory_space=pltpu.SMEM)]
        + [vmem] * (2 + len(far) + len(state)),
        out_specs=(vmem, vmem),
        scratch_shapes=[
            score_scratch(sum(part.shape[0] for part in far), rows, block),
            pltpu.VMEM((rows, block), F32),
            pltpu.VMEM((rows, block), F32),
            pltpu.VMEM((rows, value_up.shape[1]), F32),
        ],
        compiler_params=pltpu.CompilerParams(vmem_limit_bytes=32 * 2**20),
        cost_estimate=pl.CostEstimate(
            flops=4 * 10**9, bytes_accessed=14 * 10**6, transcendentals=10**6
        ),
        name="attention_far",
    )(mask, queries, *far, *state, value_up)


def own_half(blocks, core):
    half_blocks = blocks.shape[0] // 2
    return lax.dynamic_slice_in_dim(blocks, core * half_blocks, half_blocks, 0)


def after(value, event):
    one = event[(0,) * event.ndim].astype(F32) * 0.0 + 1.0
    tile = value[(slice(0, 1),) * (value.ndim - 2) + (slice(0, 16), slice(0, 128))]
    tile = (tile.astype(F32) * one).astype(value.dtype)
    return lax.dynamic_update_slice(value, tile, (0,) * value.ndim)


def gather_codes(blocks, core):
    blocks = lax.optimization_barrier(blocks)
    beside = over_ctx(blocks, AHEAD)
    side = over_ctx(own_half(blocks, core), ACROSS)
    beside_half = own_half(beside, core)
    far = over_ctx(beside_half, AHEAD)
    side_other, _ = lax.optimization_barrier((core_swap(side), beside_half))
    side_beside = over_ctx(jnp.concatenate([side, side_other], axis=0), AHEAD)
    side_far = over_ctx(far, ACROSS)
    near = (blocks, beside, core_swap(beside), side, side_other)

    def far_blocks(done):
        held = after(side_far, done)
        swapped = [core_swap(part) for part in (side_beside, far, held)]
        return (side_beside, swapped[0], far, swapped[1], held, swapped[2])

    return near, far_blocks


def store_rows(results, columns, term):
    at = 0
    for result in results:
        result[:, columns] = term[at : at + result.shape[0]].astype(BF16)
        at += result.shape[0]


def experts_kernel(count, holds, *refs):
    sources, weights_in = refs[:count], refs[count : count + 3]
    results = refs[count + 3 : 2 * count + 3]
    if holds:
        gate_weight, up_weight, down_weight, rows, sems = refs[2 * count + 3 :]
    else:
        gate_weight, up_weight, down_weight = weights_in
        (rows,) = refs[2 * count + 3 :]
    cuts = 4
    depth = rows.shape[1] // cuts
    width = depth // 2

    def weight_copy(kind, cut):
        span = slice(cut * depth, (cut + 1) * depth)
        source, target = weights_in[kind], (gate_weight, up_weight, down_weight)[kind]
        if kind == 2:
            return pltpu.make_async_copy(
                source.at[0, :, span], target.at[:, span], sems.at[kind, cut]
            )
        return pltpu.make_async_copy(source.at[0, span], target.at[span], sems.at[kind, cut])

    def arrived(kind, cut):
        if holds:
            weight_copy(kind, cut).wait()

    if holds:
        for cut in range(cuts):
            weight_copy(0, cut).start()
            weight_copy(1, cut).start()
        for cut in range(cuts):
            weight_copy(2, cut).start()
    at = 0
    for source in sources:
        rows[at : at + source.shape[0], :] = source[...]
        at += source.shape[0]
    gate_proj, up_proj = None, None
    for cut in range(cuts):
        span = slice(cut * depth, (cut + 1) * depth)
        arrived(0, cut)
        arrived(1, cut)
        gate_part = jnp.dot(rows[:, span], gate_weight[span], preferred_element_type=F32)
        up_part = jnp.dot(rows[:, span], up_weight[span], preferred_element_type=F32)
        gate_proj = gate_part if cut == 0 else gate_proj + gate_part
        up_proj = up_part if cut == 0 else up_proj + up_part
    inner_act = (gate_proj / (1.0 + jnp.exp(-gate_proj)) * up_proj).astype(BF16)
    for cut in range(cuts):
        arrived(2, cut)
        for part in range(2):
            columns = slice(cut * depth + part * width, cut * depth + (part + 1) * width)
            term = jnp.dot(inner_act, down_weight[:, columns], preferred_element_type=F32)
            store_rows(results, columns, term)


def experts_call(blocks, weights, holds, name):
    vmem = pl.BlockSpec(memory_space=pltpu.VMEM)
    anywhere = pl.BlockSpec(memory_space=pltpu.HBM)
    row_count = sum(block.shape[0] for block in blocks)
    out_shape = [jax.ShapeDtypeStruct(block.shape, BF16) for block in blocks]
    scratch = [pltpu.VMEM((row_count, blocks[0].shape[1]), BF16)]
    if holds:
        out_shape += [pltpu.VMEM(weight.shape[1:], BF16) for weight in weights]
        weights = [in_hbm(weight) for weight in weights]
        scratch.append(pltpu.SemaphoreType.DMA((3, 4)))
    found = pl.pallas_call(
        functools.partial(experts_kernel, len(blocks), holds),
        out_shape=tuple(out_shape),
        in_specs=[vmem] * len(blocks) + [anywhere if holds else vmem] * 3,
        out_specs=tuple([vmem] * len(out_shape)),
        scratch_shapes=scratch,
        compiler_params=pltpu.CompilerParams(vmem_limit_bytes=VMEM_LIMIT),
        cost_estimate=pl.CostEstimate(
            flops=15 * 10**8, bytes_accessed=15 * 10**6, transcendentals=32768
        ),
        name=name,
    )(*blocks, *weights)
    return found[: len(blocks)], found[len(blocks) :]


def gather_rows(own):
    side = over_ctx(own, ACROSS)
    ahead = over_ctx(own, AHEAD)
    back = over_ctx(own, BACK)
    far = over_ctx(ahead, AHEAD)
    side_now, _ = lax.optimization_barrier((side, ahead))
    side_ahead = over_ctx(side_now, AHEAD)
    side_back = over_ctx(side_now, BACK)
    side_far = over_ctx(far, ACROSS)
    return (ahead, back, side), (far, side_ahead, side_back, side_far)


def added(*terms):
    total = terms[0].astype(F32)
    for term in terms[1:]:
        total = total + term.astype(F32)
    return total.astype(BF16)


def reduce_rows(own, near, far):
    ahead, back, side = near
    far, side_ahead, side_back, side_far = far
    side_far_in = over_ctx(side_far, ACROSS)
    side_ahead_in = over_ctx(side_ahead, BACK)
    side_back_in = over_ctx(side_back, AHEAD)
    far_in = over_ctx(added(far, side_far_in), BACK)
    side_in = over_ctx(added(side, side_ahead_in, side_back_in), ACROSS)
    back_in = over_ctx(back, AHEAD)
    ahead_in = over_ctx(added(ahead, far_in), BACK)
    return added(own, back_in, side_in, ahead_in)


def on_device(
    queries,
    prior_codes,
    fresh_codes,
    prior_powers,
    fresh_powers,
    block_mask,
    value_up,
    output_weight,
    residual,
    norm_gain,
    router,
    route_ids,
    gate_weight,
    up_weight,
    down_weight,
):
    core = lax.axis_index("exp") % CORES
    rows_block, head_count, key_width = queries.shape
    prior_blocks = prior_powers.shape[0]
    scales = power_two(jnp.concatenate([prior_powers, fresh_powers], axis=0))
    blocks_here = jnp.concatenate(
        [jnp.transpose(prior_codes), jnp.transpose(fresh_codes)], axis=1
    ).reshape(key_width, prior_blocks + 1, rows_block)
    blocks_here = jnp.transpose(blocks_here, (1, 0, 2)).astype(F32)
    blocks_here = (blocks_here * scales[:, None, None]).astype(BF16)
    near, far_blocks = gather_codes(blocks_here, core)
    groups = rows_block // 16
    split = queries.reshape(groups, 2, 8, head_count, key_width)
    first = jnp.where(core == 0, split[:, 0], split[:, 1])
    second = jnp.where(core == 0, split[:, 1], split[:, 0])
    ordered = jnp.stack([first, second], axis=0)
    ordered = jnp.transpose(ordered, (3, 0, 1, 2, 4)).reshape(head_count * rows_block, key_width)

    state = near_call(block_mask, ordered, near, value_up, output_weight)
    *state, done = state
    far = far_blocks(done)
    keep, send = far_call(block_mask, ordered, far, state, value_up)
    expert_count = router.shape[1]
    token_count, route_count = route_ids.shape
    capacity = token_count * route_count * 2 // expert_count
    route_hits = route_ids[:, :, None] == jnp.arange(expert_count)[None, None, :]
    flat_hits = route_hits.reshape(token_count * route_count, expert_count).astype(jnp.int32)
    before = jnp.cumsum(flat_hits, axis=0) - flat_hits
    slot_index = jnp.sum(before * flat_hits, axis=1)
    target = route_ids.reshape(-1) * capacity + slot_index
    placing = (target[None, :] == jnp.arange(expert_count * capacity)[:, None]).astype(BF16)
    placing_back = jnp.transpose(placing)
    gain = norm_gain.astype(F32)
    keep, send, placing, placing_back, route_ids, gain = lax.optimization_barrier(
        (keep, send, placing, placing_back, route_ids, gain)
    )
    paired = added(keep, core_swap(send))
    model_width = residual.shape[1]
    pieces = lax.all_to_all(
        paired.reshape(groups, 8, model_width),
        "exp",
        split_axis=0,
        concat_axis=0,
        tiled=True,
        axis_index_groups=SAME_CORE,
    )
    attention = jnp.sum(pieces.astype(F32), axis=0)
    hidden = (residual.astype(F32) + attention).astype(BF16)
    hidden_wide = hidden.astype(F32)
    normed = (
        hidden_wide
        * lax.rsqrt(jnp.mean(hidden_wide * hidden_wide, axis=1, keepdims=True) + 1e-06)
        * gain
    ).astype(BF16)
    affinity = jax.nn.sigmoid(jnp.dot(normed, router, preferred_element_type=F32))
    route_hits = route_ids[:, :, None] == jnp.arange(expert_count)[None, None, :]
    chosen = jnp.sum(jnp.where(route_hits, affinity[:, None, :], 0.0), axis=2)
    gate_values = 2.5 * chosen / jnp.sum(chosen, axis=1, keepdims=True)
    repeated = jnp.repeat(normed, route_count, axis=0)
    buffer = jnp.dot(placing, repeated, preferred_element_type=F32).astype(BF16)
    sectioned = lax.all_to_all(
        buffer.reshape(expert_count, capacity, model_width),
        "exp",
        split_axis=0,
        concat_axis=0,
        tiled=True,
    )
    own_rows = sectioned.reshape(expert_count * capacity, model_width)
    near_rows, far_rows = gather_rows(own_rows)
    near_terms, weights = experts_call(
        (own_rows,) + near_rows, (gate_weight, up_weight, down_weight), True, "experts_near"
    )
    far_terms, _ = experts_call(far_rows, weights, False, "experts_far")
    summed = reduce_rows(near_terms[0], near_terms[1:], far_terms)
    summed, gate_values, hidden = lax.optimization_barrier((summed, gate_values, hidden))
    returned = lax.all_to_all(
        summed.reshape(expert_count, capacity, model_width),
        "exp",
        split_axis=0,
        concat_axis=0,
        tiled=True,
    ).reshape(expert_count * capacity, model_width)
    gathered_back = jnp.dot(
        placing_back, returned, preferred_element_type=F32
    ).reshape(token_count, route_count, model_width)
    expert_mix = jnp.sum(gate_values[:, :, None] * gathered_back, axis=1)
    return (hidden.astype(F32) + expert_mix).astype(BF16)


def solution(mesh):
    in_specs = (
        P("ctx", "exp", None),
        P("ctx", None),
        P("ctx", None),
        P("ctx"),
        P("ctx"),
        P(),
        P("exp", None, None),
        P("exp", None),
        P(("ctx", "exp"), None),
        P(),
        P(),
        P(("ctx", "exp"), None),
        P("exp", None, "ctx"),
        P("exp", None, "ctx"),
        P("exp", "ctx", None),
    )
    out_specs = P(("ctx", "exp"), None)
    return jax.shard_map(
        on_device, mesh=mesh, in_specs=in_specs, out_specs=out_specs, check_vma=False
    )
```

```python
import functools

import jax
import jax.numpy as jnp
from jax import lax
from jax.experimental import pallas as pl
from jax.experimental.pallas import tpu as pltpu
from jax.sharding import PartitionSpec as P

ROPE = 64
NOPE = 128
Y_HI, Z, Y_LO, X, CORES = 2, 4, 2, 4, 2
STEP_BLOCKS = 4
VMEM_LIMIT = 36 * 2**20
HEADS_HERE = 4
F32 = jnp.float32
BF16 = jnp.bfloat16


def ctx_pairs(move):
    pairs = []
    for y in range(Y_HI):
        for z in range(Z):
            for i in range(Y_LO * X * CORES):
                to_y, to_z = move(y, z, 1 - 2 * (i % CORES))
                pairs.append(
                    (
                        (y * Z + z) * Y_LO * X * CORES + i,
                        (to_y * Z + to_z) * Y_LO * X * CORES + i,
                    )
                )
    return pairs


AHEAD = ctx_pairs(lambda y, z, way: (y, (z + way) % Z))
BACK = ctx_pairs(lambda y, z, way: (y, (z - way) % Z))
OPPOSITE = ctx_pairs(lambda y, z, way: (y, (z + 2) % Z))
ACROSS = ctx_pairs(lambda y, z, way: (1 - y, z))
CORE_SWAP = [(i, i ^ 1) for i in range(Y_LO * X * CORES)]
SAME_CORE = [[2 * i + core for i in range(Y_LO * X)] for core in range(CORES)]


def over_ctx(value, pairs):
    return lax.ppermute(value, ("ctx", "exp"), pairs)


def core_swap(value):
    return lax.ppermute(value, "exp", CORE_SWAP)


def power_two(powers):
    return jnp.where(powers < 0, 0.5, jnp.where(powers > 0, 2.0, 1.0)).astype(jnp.float32)


def in_hbm(value):
    return pltpu.with_memory_space_constraint(value, pltpu.HBM)


def attend(mask, queries, steps, diagonal, scores, top, total, mixture):
    rows = queries.shape[0]
    latent_width = mixture.shape[1]
    block = top.shape[1]
    factor = 1.4426950408889634 / (NOPE + ROPE) ** 0.5
    top[...] = jnp.full_like(top, -1e30)
    total[...] = jnp.zeros_like(total)
    mixture[...] = jnp.zeros_like(mixture)

    def keys_of(step, height):
        return jnp.concatenate([part[i, :height] for part, i, _ in step], axis=1)

    def lane_fold(value, fold):
        folded = value[:, :block]
        for i in range(1, STEP_BLOCKS):
            folded = fold(folded, value[:, i * block : (i + 1) * block])
        return folded

    ctx_index = lax.axis_index("ctx")
    core = lax.axis_index("exp") % CORES
    owners = mask.shape[0]
    prior_blocks = mask.shape[1] // owners - 1

    def flag(place):
        dy, dz, number = place
        owner = (ctx_index // Z + dy) % Y_HI * Z + (ctx_index % Z + dz + Z) % Z
        prior = owner * prior_blocks + jnp.minimum(number, prior_blocks - 1)
        fresh = owners * prior_blocks + owner
        return mask[ctx_index, jnp.where(number < prior_blocks, prior, fresh)]

    def flags_of(number):
        return [flag(place) for _, _, place in steps[number]]

    all_flags = [flags_of(number) for number in range(len(steps))]
    live = [(sum(flags) > 0).astype(jnp.int32) for flags in all_flags]
    straight = sum(live) >= len(steps) - 1

    def score(step, number):
        found = jnp.dot(
            queries[...], keys_of(step, queries.shape[1]), preferred_element_type=F32
        )
        column = lax.broadcasted_iota(jnp.int32, (1, STEP_BLOCKS * block), 1) // block
        shown = jnp.zeros(column.shape, jnp.int32)
        for i, flag in enumerate(all_flags[number]):
            shown = jnp.where(column == i, flag, shown)
        found = jnp.where(shown > 0, found, -1e30)
        if diagonal and number == 0:
            last = (STEP_BLOCKS - 1) * block
            seen = jnp.where(causal(), found[:, last:], -1e30)
            found = jnp.concatenate([found[:, :last], seen], axis=1)
        scores[number] = found
        top[...] = jnp.maximum(top[...], lane_fold(found, jnp.maximum))

    def causal():
        tokens = rows // HEADS_HERE
        row = lax.broadcasted_iota(jnp.int32, (rows, 1), 0) % tokens
        relative = row // (tokens // 2)
        within = row % (tokens // 2)
        side = jnp.where(relative == 0, core, 1 - core)
        token = within // 8 * 16 + side * 8 + within % 8
        return lax.broadcasted_iota(jnp.int32, (1, block), 1) <= token

    def mix(row_top, step, number):
        weights = jnp.exp2((scores[number] - row_top) * factor)
        total[...] += lane_fold(weights, jnp.add)
        mixture[...] += lax.dot_general(
            weights.astype(BF16),
            keys_of(step, latent_width),
            (((1,), (1,)), ((), ())),
            preferred_element_type=F32,
        )

    def all_steps(branches):
        def each_step(body):
            for number, step in enumerate(steps):
                if branches:
                    pl.when(live[number] > 0)(functools.partial(body, step, number))
                else:
                    body(step, number)

        each_step(score)
        row_top = jnp.max(top[...], axis=1, keepdims=True)
        each_step(functools.partial(mix, row_top))
        top[...] = jnp.broadcast_to(row_top, top.shape)

    pl.when(straight)(functools.partial(all_steps, False))
    pl.when(jnp.logical_not(straight))(functools.partial(all_steps, True))


def whole(part, dy, dz):
    return [(part, i, (dy, dz, i)) for i in range(STEP_BLOCKS)]


def halves(part, other, dy, dz, first):
    half = STEP_BLOCKS // 2
    return [
        (array, i, (dy, dz, start + i))
        for array, start in ((part, first), (other, half - first))
        for i in range(half)
    ]


def near_kernel(
    mask, queries, own, beside, beside_other, side, side_other, weight_hbm,
    top, total, mixture, weight, done, scores, weight_sem,
):
    copy = pltpu.make_async_copy(weight_hbm, weight, weight_sem)
    copy.start()
    core = lax.axis_index("exp") % CORES
    way = 1 - 2 * core
    first = core * (STEP_BLOCKS // 2)
    steps = [
        whole(own, 0, 0),
        whole(beside, 0, -way),
        whole(beside_other, 0, way),
        halves(side, side_other, 1, 0, first),
    ]
    attend(mask, queries, steps, True, scores, top, total, mixture)
    done[...] = jnp.ones_like(done)
    copy.wait()


def far_kernel(
    mask, queries, beside, beside_other, far, far_other, side_far, side_far_other,
    near_top, near_total, near_mixture, weight, value_up,
    out_keep, out_send, scores, top, total, mixture,
):
    heads = value_up.shape[0]
    tokens = queries.shape[0] // heads
    factor = 1.4426950408889634 / (NOPE + ROPE) ** 0.5
    core = lax.axis_index("exp") % CORES
    way = 1 - 2 * core
    half = STEP_BLOCKS // 2
    first = core * half

    def sent(part, dz, first):
        low = [(part, i, (1, dz, first + i)) for i in range(half)]
        return low + [(part, half + i, (1, dz, half - first + i)) for i in range(half)]

    steps = [
        sent(beside, -way, first),
        sent(beside_other, way, half - first),
        halves(far, far_other, 0, 2, first),
        halves(side_far, side_far_other, 1, 2, first),
    ]
    attend(mask, queries, steps, False, scores, top, total, mixture)
    far_top = top[:, :1]
    near_row_top = near_top[:, :1]
    both_top = jnp.maximum(near_row_top, far_top)
    near_scale = jnp.exp2((near_row_top - both_top) * factor)
    far_scale = jnp.exp2((far_top - both_top) * factor)
    row_total = jnp.sum(near_total[...] * near_scale + total[...] * far_scale, axis=1, keepdims=True)
    near_scale = near_scale / row_total
    far_scale = far_scale / row_total
    per_head = []
    for head in range(heads):
        span = slice(head * tokens, (head + 1) * tokens)
        attended = near_mixture[span] * near_scale[span] + mixture[span] * far_scale[span]
        per_head.append(
            jnp.dot(
                attended.astype(BF16), value_up[head], preferred_element_type=F32
            ).astype(BF16)
        )
    flat_heads = jnp.concatenate(per_head, axis=1)
    out_width = 1024
    half = tokens // 2

    for step in range(weight.shape[1] // out_width):
        columns = slice(step * out_width, (step + 1) * out_width)
        term = jnp.dot(flat_heads, weight[:, columns], preferred_element_type=F32)
        out_keep[:, columns] = term[:half].astype(BF16)
        out_send[:, columns] = term[half:].astype(BF16)


def score_scratch(blocks, rows, block):
    return pltpu.VMEM((blocks // STEP_BLOCKS, rows, STEP_BLOCKS * block), F32)


def near_call(mask, queries, near, value_up, output_weight):
    rows, block = queries.shape[0], near[0].shape[2]
    vmem = pl.BlockSpec(memory_space=pltpu.VMEM)
    lanes = jax.ShapeDtypeStruct((rows, block), F32)
    return pl.pallas_call(
        near_kernel,
        out_shape=(
            lanes,
            lanes,
            jax.ShapeDtypeStruct((rows, value_up.shape[1]), F32),
            pltpu.VMEM(output_weight.shape, BF16),
            jax.ShapeDtypeStruct((8, block), F32),
        ),
        in_specs=[pl.BlockSpec(memory_space=pltpu.SMEM)]
        + [vmem] * (1 + len(near))
        + [pl.BlockSpec(memory_space=pltpu.HBM)],
        out_specs=(vmem,) * 5,
        scratch_shapes=[
            score_scratch(sum(part.shape[0] for part in near), rows, block),
            pltpu.SemaphoreType.DMA,
        ],
        compiler_params=pltpu.CompilerParams(vmem_limit_bytes=32 * 2**20),
        cost_estimate=pl.CostEstimate(
            flops=3 * 10**9, bytes_accessed=12 * 10**6, transcendentals=10**6
        ),
        name="attention_near",
    )(mask, queries, *near, in_hbm(output_weight))


def far_call(mask, queries, far, state, value_up):
    rows, block = queries.shape[0], far[0].shape[2]
    tokens = rows // value_up.shape[0]
    vmem = pl.BlockSpec(memory_space=pltpu.VMEM)
    out = jax.ShapeDtypeStruct((tokens // 2, state[3].shape[1]), BF16)
    return pl.pallas_call(
        far_kernel,
        out_shape=(out, out),
        in_specs=[pl.BlockSpec(memory_space=pltpu.SMEM)]
        + [vmem] * (2 + len(far) + len(state)),
        out_specs=(vmem, vmem),
        scratch_shapes=[
            score_scratch(sum(part.shape[0] for part in far), rows, block),
            pltpu.VMEM((rows, block), F32),
            pltpu.VMEM((rows, block), F32),
            pltpu.VMEM((rows, value_up.shape[1]), F32),
        ],
        compiler_params=pltpu.CompilerParams(vmem_limit_bytes=32 * 2**20),
        cost_estimate=pl.CostEstimate(
            flops=4 * 10**9, bytes_accessed=14 * 10**6, transcendentals=10**6
        ),
        name="attention_far",
    )(mask, queries, *far, *state, value_up)


def own_half(blocks, core):
    half_blocks = blocks.shape[0] // 2
    return lax.dynamic_slice_in_dim(blocks, core * half_blocks, half_blocks, 0)


def after(value, event):
    one = event[(0,) * event.ndim].astype(F32) * 0.0 + 1.0
    tile = value[(slice(0, 1),) * (value.ndim - 2) + (slice(0, 16), slice(0, 128))]
    tile = (tile.astype(F32) * one).astype(value.dtype)
    return lax.dynamic_update_slice(value, tile, (0,) * value.ndim)


def gather_codes(blocks, core):
    blocks = lax.optimization_barrier(blocks)
    beside = over_ctx(blocks, AHEAD)
    side = over_ctx(own_half(blocks, core), ACROSS)
    beside_half = own_half(beside, core)
    far = over_ctx(beside_half, AHEAD)
    side_other, _ = lax.optimization_barrier((core_swap(side), beside_half))
    side_beside = over_ctx(jnp.concatenate([side, side_other], axis=0), AHEAD)
    side_far = over_ctx(far, ACROSS)
    near = (blocks, beside, core_swap(beside), side, side_other)

    def far_blocks(done):
        held = after(side_far, done)
        swapped = [core_swap(part) for part in (side_beside, far, held)]
        return (side_beside, swapped[0], far, swapped[1], held, swapped[2])

    return near, far_blocks


def store_rows(results, columns, term):
    at = 0
    for result in results:
        result[:, columns] = term[at : at + result.shape[0]].astype(BF16)
        at += result.shape[0]


def experts_kernel(count, holds, *refs):
    sources, weights_in = refs[:count], refs[count : count + 3]
    results = refs[count + 3 : 2 * count + 3]
    if holds:
        gate_weight, up_weight, down_weight, rows, sems = refs[2 * count + 3 :]
    else:
        gate_weight, up_weight, down_weight = weights_in
        (rows,) = refs[2 * count + 3 :]
    cuts = 4
    depth = rows.shape[1] // cuts
    width = depth // 2

    def weight_copy(kind, cut):
        span = slice(cut * depth, (cut + 1) * depth)
        source, target = weights_in[kind], (gate_weight, up_weight, down_weight)[kind]
        if kind == 2:
            return pltpu.make_async_copy(
                source.at[0, :, span], target.at[:, span], sems.at[kind, cut]
            )
        return pltpu.make_async_copy(source.at[0, span], target.at[span], sems.at[kind, cut])

    def arrived(kind, cut):
        if holds:
            weight_copy(kind, cut).wait()

    if holds:
        for cut in range(cuts):
            weight_copy(0, cut).start()
            weight_copy(1, cut).start()
        for cut in range(cuts):
            weight_copy(2, cut).start()
    at = 0
    for source in sources:
        rows[at : at + source.shape[0], :] = source[...]
        at += source.shape[0]
    gate_proj, up_proj = None, None
    for cut in range(cuts):
        span = slice(cut * depth, (cut + 1) * depth)
        arrived(0, cut)
        arrived(1, cut)
        gate_part = jnp.dot(rows[:, span], gate_weight[span], preferred_element_type=F32)
        up_part = jnp.dot(rows[:, span], up_weight[span], preferred_element_type=F32)
        gate_proj = gate_part if cut == 0 else gate_proj + gate_part
        up_proj = up_part if cut == 0 else up_proj + up_part
    inner_act = (gate_proj / (1.0 + jnp.exp(-gate_proj)) * up_proj).astype(BF16)
    for cut in range(cuts):
        arrived(2, cut)
        for part in range(2):
            columns = slice(cut * depth + part * width, cut * depth + (part + 1) * width)
            term = jnp.dot(inner_act, down_weight[:, columns], preferred_element_type=F32)
            store_rows(results, columns, term)


def experts_call(blocks, weights, holds, name):
    vmem = pl.BlockSpec(memory_space=pltpu.VMEM)
    anywhere = pl.BlockSpec(memory_space=pltpu.HBM)
    row_count = sum(block.shape[0] for block in blocks)
    out_shape = [jax.ShapeDtypeStruct(block.shape, BF16) for block in blocks]
    scratch = [pltpu.VMEM((row_count, blocks[0].shape[1]), BF16)]
    if holds:
        out_shape += [pltpu.VMEM(weight.shape[1:], BF16) for weight in weights]
        weights = [in_hbm(weight) for weight in weights]
        scratch.append(pltpu.SemaphoreType.DMA((3, 4)))
    found = pl.pallas_call(
        functools.partial(experts_kernel, len(blocks), holds),
        out_shape=tuple(out_shape),
        in_specs=[vmem] * len(blocks) + [anywhere if holds else vmem] * 3,
        out_specs=tuple([vmem] * len(out_shape)),
        scratch_shapes=scratch,
        compiler_params=pltpu.CompilerParams(vmem_limit_bytes=VMEM_LIMIT),
        cost_estimate=pl.CostEstimate(
            flops=15 * 10**8, bytes_accessed=15 * 10**6, transcendentals=32768
        ),
        name=name,
    )(*blocks, *weights)
    return found[: len(blocks)], found[len(blocks) :]


def gather_rows(own):
    far = over_ctx(own, OPPOSITE)
    side = over_ctx(own, ACROSS)
    ahead = over_ctx(own, AHEAD)
    back = over_ctx(own, BACK)
    side_ahead = over_ctx(side, AHEAD)
    side_back = over_ctx(side, BACK)
    side_far = over_ctx(far, ACROSS)
    return (ahead, back, side), (far, side_ahead, side_back, side_far)


def added(*terms):
    total = terms[0].astype(F32)
    for term in terms[1:]:
        total = total + term.astype(F32)
    return total.astype(BF16)


def reduce_rows(own, near, far):
    ahead, back, side = near
    far, side_ahead, side_back, side_far = far
    side_far_in = over_ctx(side_far, ACROSS)
    side_ahead_in = over_ctx(side_ahead, BACK)
    side_back_in = over_ctx(side_back, AHEAD)
    side_in = over_ctx(added(side, side_ahead_in, side_back_in), ACROSS)
    far_in = over_ctx(added(far, side_far_in), OPPOSITE)
    ahead_in = over_ctx(ahead, BACK)
    back_in = over_ctx(back, AHEAD)
    return added(own, ahead_in, back_in, side_in, far_in)


def on_device(
    queries,
    prior_codes,
    fresh_codes,
    prior_powers,
    fresh_powers,
    block_mask,
    value_up,
    output_weight,
    residual,
    norm_gain,
    router,
    route_ids,
    gate_weight,
    up_weight,
    down_weight,
):
    core = lax.axis_index("exp") % CORES
    rows_block, head_count, key_width = queries.shape
    prior_blocks = prior_powers.shape[0]
    scales = power_two(jnp.concatenate([prior_powers, fresh_powers], axis=0))
    blocks_here = jnp.concatenate(
        [jnp.transpose(prior_codes), jnp.transpose(fresh_codes)], axis=1
    ).reshape(key_width, prior_blocks + 1, rows_block)
    blocks_here = jnp.transpose(blocks_here, (1, 0, 2)).astype(F32)
    blocks_here = (blocks_here * scales[:, None, None]).astype(BF16)
    near, far_blocks = gather_codes(blocks_here, core)
    groups = rows_block // 16
    split = queries.reshape(groups, 2, 8, head_count, key_width)
    first = jnp.where(core == 0, split[:, 0], split[:, 1])
    second = jnp.where(core == 0, split[:, 1], split[:, 0])
    ordered = jnp.stack([first, second], axis=0)
    ordered = jnp.transpose(ordered, (3, 0, 1, 2, 4)).reshape(head_count * rows_block, key_width)

    state = near_call(block_mask, ordered, near, value_up, output_weight)
    *state, done = state
    far = far_blocks(done)
    keep, send = far_call(block_mask, ordered, far, state, value_up)
    expert_count = router.shape[1]
    token_count, route_count = route_ids.shape
    capacity = token_count * route_count * 2 // expert_count
    route_hits = route_ids[:, :, None] == jnp.arange(expert_count)[None, None, :]
    flat_hits = route_hits.reshape(token_count * route_count, expert_count).astype(jnp.int32)
    before = jnp.cumsum(flat_hits, axis=0) - flat_hits
    slot_index = jnp.sum(before * flat_hits, axis=1)
    target = route_ids.reshape(-1) * capacity + slot_index
    placing = (target[None, :] == jnp.arange(expert_count * capacity)[:, None]).astype(BF16)
    placing_back = jnp.transpose(placing)
    gain = norm_gain.astype(F32)
    keep, send, placing, placing_back, route_ids, gain = lax.optimization_barrier(
        (keep, send, placing, placing_back, route_ids, gain)
    )
    paired = added(keep, core_swap(send))
    model_width = residual.shape[1]
    pieces = lax.all_to_all(
        paired.reshape(groups, 8, model_width),
        "exp",
        split_axis=0,
        concat_axis=0,
        tiled=True,
        axis_index_groups=SAME_CORE,
    )
    attention = jnp.sum(pieces.astype(F32), axis=0)
    hidden = (residual.astype(F32) + attention).astype(BF16)
    hidden_wide = hidden.astype(F32)
    normed = (
        hidden_wide
        * lax.rsqrt(jnp.mean(hidden_wide * hidden_wide, axis=1, keepdims=True) + 1e-06)
        * gain
    ).astype(BF16)
    affinity = jax.nn.sigmoid(jnp.dot(normed, router, preferred_element_type=F32))
    route_hits = route_ids[:, :, None] == jnp.arange(expert_count)[None, None, :]
    chosen = jnp.sum(jnp.where(route_hits, affinity[:, None, :], 0.0), axis=2)
    gate_values = 2.5 * chosen / jnp.sum(chosen, axis=1, keepdims=True)
    repeated = jnp.repeat(normed, route_count, axis=0)
    buffer = jnp.dot(placing, repeated, preferred_element_type=F32).astype(BF16)
    sectioned = lax.all_to_all(
        buffer.reshape(expert_count, capacity, model_width),
        "exp",
        split_axis=0,
        concat_axis=0,
        tiled=True,
    )
    own_rows = sectioned.reshape(expert_count * capacity, model_width)
    near_rows, far_rows = gather_rows(own_rows)
    near_terms, weights = experts_call(
        (own_rows,) + near_rows, (gate_weight, up_weight, down_weight), True, "experts_near"
    )
    far_terms, _ = experts_call(far_rows, weights, False, "experts_far")
    summed = reduce_rows(near_terms[0], near_terms[1:], far_terms)
    summed, gate_values, hidden = lax.optimization_barrier((summed, gate_values, hidden))
    returned = lax.all_to_all(
        summed.reshape(expert_count, capacity, model_width),
        "exp",
        split_axis=0,
        concat_axis=0,
        tiled=True,
    ).reshape(expert_count * capacity, model_width)
    gathered_back = jnp.dot(
        placing_back, returned, preferred_element_type=F32
    ).reshape(token_count, route_count, model_width)
    expert_mix = jnp.sum(gate_values[:, :, None] * gathered_back, axis=1)
    return (hidden.astype(F32) + expert_mix).astype(BF16)


def solution(mesh):
    in_specs = (
        P("ctx", "exp", None),
        P("ctx", None),
        P("ctx", None),
        P("ctx"),
        P("ctx"),
        P(),
        P("exp", None, None),
        P("exp", None),
        P(("ctx", "exp"), None),
        P(),
        P(),
        P(("ctx", "exp"), None),
        P("exp", None, "ctx"),
        P("exp", None, "ctx"),
        P("exp", "ctx", None),
    )
    out_specs = P(("ctx", "exp"), None)
    return jax.shard_map(
        on_device, mesh=mesh, in_specs=in_specs, out_specs=out_specs, check_vma=False
    )
```

```python
import functools

import jax
import jax.numpy as jnp
from jax import lax
from jax.experimental import pallas as pl
from jax.experimental.pallas import tpu as pltpu
from jax.sharding import PartitionSpec as P

ROPE = 64
NOPE = 128
Y_HI, Z, Y_LO, X, CORES = 2, 4, 2, 4, 2
STEP_BLOCKS = 4
VMEM_LIMIT = 36 * 2**20
HEADS_HERE = 4
F32 = jnp.float32
BF16 = jnp.bfloat16


def ctx_pairs(move):
    pairs = []
    for y in range(Y_HI):
        for z in range(Z):
            for i in range(Y_LO * X * CORES):
                to_y, to_z = move(y, z, 1 - 2 * (i % CORES))
                pairs.append(
                    (
                        (y * Z + z) * Y_LO * X * CORES + i,
                        (to_y * Z + to_z) * Y_LO * X * CORES + i,
                    )
                )
    return pairs


AHEAD = ctx_pairs(lambda y, z, way: (y, (z + way) % Z))
BACK = ctx_pairs(lambda y, z, way: (y, (z - way) % Z))
OPPOSITE = ctx_pairs(lambda y, z, way: (y, (z + 2) % Z))
ACROSS = ctx_pairs(lambda y, z, way: (1 - y, z))
CORE_SWAP = [(i, i ^ 1) for i in range(Y_LO * X * CORES)]
SAME_CORE = [[2 * i + core for i in range(Y_LO * X)] for core in range(CORES)]


def over_ctx(value, pairs):
    return lax.ppermute(value, ("ctx", "exp"), pairs)


def core_swap(value):
    return lax.ppermute(value, "exp", CORE_SWAP)


def power_two(powers):
    return jnp.where(powers < 0, 0.5, jnp.where(powers > 0, 2.0, 1.0)).astype(jnp.float32)


def in_hbm(value):
    return pltpu.with_memory_space_constraint(value, pltpu.HBM)


def attend(mask, queries, steps, diagonal, scores, top, total, mixture):
    rows = queries.shape[0]
    latent_width = mixture.shape[1]
    block = top.shape[1]
    factor = 1.4426950408889634 / (NOPE + ROPE) ** 0.5

    def keys_of(step, height):
        return jnp.concatenate([part[i, :height] for part, i, _ in step], axis=1)

    def lane_fold(value, fold):
        folded = value[:, :block]
        for i in range(1, STEP_BLOCKS):
            folded = fold(folded, value[:, i * block : (i + 1) * block])
        return folded

    ctx_index = lax.axis_index("ctx")
    core = lax.axis_index("exp") % CORES
    owners = mask.shape[0]
    prior_blocks = mask.shape[1] // owners - 1

    def flag(place):
        dy, dz, number = place
        owner = (ctx_index // Z + dy) % Y_HI * Z + (ctx_index % Z + dz + Z) % Z
        prior = owner * prior_blocks + jnp.minimum(number, prior_blocks - 1)
        fresh = owners * prior_blocks + owner
        return mask[ctx_index, jnp.where(number < prior_blocks, prior, fresh)]

    def flags_of(number):
        return [flag(place) for _, _, place in steps[number]]

    all_flags = [flags_of(number) for number in range(len(steps))]
    live = [(sum(flags) > 0).astype(jnp.int32) for flags in all_flags]
    straight = sum(live) >= len(steps) - 1

    def score(step, number, first):
        found = jnp.dot(
            queries[...], keys_of(step, queries.shape[1]), preferred_element_type=F32
        )
        column = lax.broadcasted_iota(jnp.int32, (1, STEP_BLOCKS * block), 1) // block
        shown = jnp.zeros(column.shape, jnp.int32)
        for i, flag in enumerate(all_flags[number]):
            shown = jnp.where(column == i, flag, shown)
        found = jnp.where(shown > 0, found, -1e30)
        if diagonal and number == 0:
            last = (STEP_BLOCKS - 1) * block
            seen = jnp.where(causal(), found[:, last:], -1e30)
            found = jnp.concatenate([found[:, :last], seen], axis=1)
        scores[number] = found
        found_top = lane_fold(found, jnp.maximum)
        top[...] = found_top if first else jnp.maximum(top[...], found_top)

    def causal():
        tokens = rows // HEADS_HERE
        row = lax.broadcasted_iota(jnp.int32, (rows, 1), 0) % tokens
        relative = row // (tokens // 2)
        within = row % (tokens // 2)
        side = jnp.where(relative == 0, core, 1 - core)
        token = within // 8 * 16 + side * 8 + within % 8
        return lax.broadcasted_iota(jnp.int32, (1, block), 1) <= token

    def mix(row_top, step, number, first):
        weights = jnp.exp2((scores[number] - row_top) * factor)
        found_total = lane_fold(weights, jnp.add)
        found_mixture = lax.dot_general(
            weights.astype(BF16),
            keys_of(step, latent_width),
            (((1,), (1,)), ((), ())),
            preferred_element_type=F32,
        )
        total[...] = found_total if first else total[...] + found_total
        mixture[...] = found_mixture if first else mixture[...] + found_mixture

    def all_steps(branches):
        if branches:
            top[...] = jnp.full_like(top, -1e30)
            total[...] = jnp.zeros_like(total)
            mixture[...] = jnp.zeros_like(mixture)

        def each_step(body):
            for number, step in enumerate(steps):
                if branches:
                    pl.when(live[number] > 0)(functools.partial(body, step, number, False))
                else:
                    body(step, number, number == 0)

        each_step(score)
        row_top = jnp.max(top[...], axis=1, keepdims=True)
        each_step(functools.partial(mix, row_top))
        top[...] = jnp.broadcast_to(row_top, top.shape)

    pl.when(straight)(functools.partial(all_steps, False))
    pl.when(jnp.logical_not(straight))(functools.partial(all_steps, True))


def whole(part, dy, dz):
    return [(part, i, (dy, dz, i)) for i in range(STEP_BLOCKS)]


def halves(part, other, dy, dz, first):
    half = STEP_BLOCKS // 2
    return [
        (array, i, (dy, dz, start + i))
        for array, start in ((part, first), (other, half - first))
        for i in range(half)
    ]


def near_kernel(
    mask, queries, own, beside, beside_other, side, side_other, weight_hbm,
    top, total, mixture, weight, done, scores, weight_sem,
):
    copy = pltpu.make_async_copy(weight_hbm, weight, weight_sem)
    copy.start()
    core = lax.axis_index("exp") % CORES
    way = 1 - 2 * core
    first = core * (STEP_BLOCKS // 2)
    steps = [
        whole(own, 0, 0),
        whole(beside, 0, -way),
        whole(beside_other, 0, way),
        halves(side, side_other, 1, 0, first),
    ]
    attend(mask, queries, steps, True, scores, top, total, mixture)
    done[...] = jnp.ones_like(done)
    copy.wait()


def far_kernel(
    mask, queries, beside, beside_other, far, far_other, side_far, side_far_other,
    near_top, near_total, near_mixture, weight, value_up,
    out_keep, out_send, scores, top, total, mixture,
):
    heads = value_up.shape[0]
    tokens = queries.shape[0] // heads
    factor = 1.4426950408889634 / (NOPE + ROPE) ** 0.5
    core = lax.axis_index("exp") % CORES
    way = 1 - 2 * core
    half = STEP_BLOCKS // 2
    first = core * half

    def sent(part, dz, first):
        low = [(part, i, (1, dz, first + i)) for i in range(half)]
        return low + [(part, half + i, (1, dz, half - first + i)) for i in range(half)]

    steps = [
        sent(beside, -way, first),
        sent(beside_other, way, half - first),
        halves(far, far_other, 0, 2, first),
        halves(side_far, side_far_other, 1, 2, first),
    ]
    attend(mask, queries, steps, False, scores, top, total, mixture)
    far_top = top[:, :1]
    near_row_top = near_top[:, :1]
    both_top = jnp.maximum(near_row_top, far_top)
    near_scale = jnp.exp2((near_row_top - both_top) * factor)
    far_scale = jnp.exp2((far_top - both_top) * factor)
    row_total = jnp.sum(near_total[...] * near_scale + total[...] * far_scale, axis=1, keepdims=True)
    near_scale = near_scale / row_total
    far_scale = far_scale / row_total
    per_head = []
    for head in range(heads):
        span = slice(head * tokens, (head + 1) * tokens)
        attended = near_mixture[span] * near_scale[span] + mixture[span] * far_scale[span]
        per_head.append(
            jnp.dot(
                attended.astype(BF16), value_up[head], preferred_element_type=F32
            ).astype(BF16)
        )
    flat_heads = jnp.concatenate(per_head, axis=1)
    out_width = 1024
    half = tokens // 2

    for step in range(weight.shape[1] // out_width):
        columns = slice(step * out_width, (step + 1) * out_width)
        term = jnp.dot(flat_heads, weight[:, columns], preferred_element_type=F32)
        out_keep[:, columns] = term[:half].astype(BF16)
        out_send[:, columns] = term[half:].astype(BF16)


def score_scratch(blocks, rows, block):
    return pltpu.VMEM((blocks // STEP_BLOCKS, rows, STEP_BLOCKS * block), F32)


def near_call(mask, queries, near, value_up, output_weight):
    rows, block = queries.shape[0], near[0].shape[2]
    vmem = pl.BlockSpec(memory_space=pltpu.VMEM)
    lanes = jax.ShapeDtypeStruct((rows, block), F32)
    return pl.pallas_call(
        near_kernel,
        out_shape=(
            lanes,
            lanes,
            jax.ShapeDtypeStruct((rows, value_up.shape[1]), F32),
            pltpu.VMEM(output_weight.shape, BF16),
            jax.ShapeDtypeStruct((8, block), F32),
        ),
        in_specs=[pl.BlockSpec(memory_space=pltpu.SMEM)]
        + [vmem] * (1 + len(near))
        + [pl.BlockSpec(memory_space=pltpu.HBM)],
        out_specs=(vmem,) * 5,
        scratch_shapes=[
            score_scratch(sum(part.shape[0] for part in near), rows, block),
            pltpu.SemaphoreType.DMA,
        ],
        compiler_params=pltpu.CompilerParams(vmem_limit_bytes=32 * 2**20),
        cost_estimate=pl.CostEstimate(
            flops=3 * 10**9, bytes_accessed=12 * 10**6, transcendentals=10**6
        ),
        name="attention_near",
    )(mask, queries, *near, in_hbm(output_weight))


def far_call(mask, queries, far, state, value_up):
    rows, block = queries.shape[0], far[0].shape[2]
    tokens = rows // value_up.shape[0]
    vmem = pl.BlockSpec(memory_space=pltpu.VMEM)
    out = jax.ShapeDtypeStruct((tokens // 2, state[3].shape[1]), BF16)
    return pl.pallas_call(
        far_kernel,
        out_shape=(out, out),
        in_specs=[pl.BlockSpec(memory_space=pltpu.SMEM)]
        + [vmem] * (2 + len(far) + len(state)),
        out_specs=(vmem, vmem),
        scratch_shapes=[
            score_scratch(sum(part.shape[0] for part in far), rows, block),
            pltpu.VMEM((rows, block), F32),
            pltpu.VMEM((rows, block), F32),
            pltpu.VMEM((rows, value_up.shape[1]), F32),
        ],
        compiler_params=pltpu.CompilerParams(vmem_limit_bytes=32 * 2**20),
        cost_estimate=pl.CostEstimate(
            flops=4 * 10**9, bytes_accessed=14 * 10**6, transcendentals=10**6
        ),
        name="attention_far",
    )(mask, queries, *far, *state, value_up)


def own_half(blocks, core):
    half_blocks = blocks.shape[0] // 2
    return lax.dynamic_slice_in_dim(blocks, core * half_blocks, half_blocks, 0)


def after(value, event):
    one = event[(0,) * event.ndim].astype(F32) * 0.0 + 1.0
    tile = value[(slice(0, 1),) * (value.ndim - 2) + (slice(0, 16), slice(0, 128))]
    tile = (tile.astype(F32) * one).astype(value.dtype)
    return lax.dynamic_update_slice(value, tile, (0,) * value.ndim)


def gather_codes(blocks, core):
    blocks = lax.optimization_barrier(blocks)
    beside = over_ctx(blocks, AHEAD)
    side = over_ctx(own_half(blocks, core), ACROSS)
    beside_half = own_half(beside, core)
    far = over_ctx(beside_half, AHEAD)
    side_other, _ = lax.optimization_barrier((core_swap(side), beside_half))
    side_beside = over_ctx(jnp.concatenate([side, side_other], axis=0), AHEAD)
    side_far = over_ctx(far, ACROSS)
    near = (blocks, beside, core_swap(beside), side, side_other)

    def far_blocks(done):
        held = after(side_far, done)
        swapped = [core_swap(part) for part in (side_beside, far, held)]
        return (side_beside, swapped[0], far, swapped[1], held, swapped[2])

    return near, far_blocks


def store_rows(results, columns, term):
    at = 0
    for result in results:
        result[:, columns] = term[at : at + result.shape[0]].astype(BF16)
        at += result.shape[0]


def experts_kernel(count, holds, *refs):
    sources, weights_in = refs[:count], refs[count : count + 3]
    results = refs[count + 3 : 2 * count + 3]
    if holds:
        gate_weight, up_weight, down_weight, rows, sems = refs[2 * count + 3 :]
    else:
        gate_weight, up_weight, down_weight = weights_in
        (rows,) = refs[2 * count + 3 :]
    cuts = 4
    depth = rows.shape[1] // cuts
    width = depth // 2

    def weight_copy(kind, cut):
        span = slice(cut * depth, (cut + 1) * depth)
        source, target = weights_in[kind], (gate_weight, up_weight, down_weight)[kind]
        if kind == 2:
            return pltpu.make_async_copy(
                source.at[0, :, span], target.at[:, span], sems.at[kind, cut]
            )
        return pltpu.make_async_copy(source.at[0, span], target.at[span], sems.at[kind, cut])

    def arrived(kind, cut):
        if holds:
            weight_copy(kind, cut).wait()

    if holds:
        for cut in range(cuts):
            weight_copy(0, cut).start()
            weight_copy(1, cut).start()
        for cut in range(cuts):
            weight_copy(2, cut).start()
    at = 0
    for source in sources:
        rows[at : at + source.shape[0], :] = source[...]
        at += source.shape[0]
    gate_proj, up_proj = None, None
    for cut in range(cuts):
        span = slice(cut * depth, (cut + 1) * depth)
        arrived(0, cut)
        arrived(1, cut)
        gate_part = jnp.dot(rows[:, span], gate_weight[span], preferred_element_type=F32)
        up_part = jnp.dot(rows[:, span], up_weight[span], preferred_element_type=F32)
        gate_proj = gate_part if cut == 0 else gate_proj + gate_part
        up_proj = up_part if cut == 0 else up_proj + up_part
    inner_act = (gate_proj / (1.0 + jnp.exp(-gate_proj)) * up_proj).astype(BF16)
    for cut in range(cuts):
        arrived(2, cut)
        for part in range(2):
            columns = slice(cut * depth + part * width, cut * depth + (part + 1) * width)
            term = jnp.dot(inner_act, down_weight[:, columns], preferred_element_type=F32)
            store_rows(results, columns, term)


def experts_call(blocks, weights, holds, name):
    vmem = pl.BlockSpec(memory_space=pltpu.VMEM)
    anywhere = pl.BlockSpec(memory_space=pltpu.HBM)
    row_count = sum(block.shape[0] for block in blocks)
    out_shape = [jax.ShapeDtypeStruct(block.shape, BF16) for block in blocks]
    scratch = [pltpu.VMEM((row_count, blocks[0].shape[1]), BF16)]
    if holds:
        out_shape += [pltpu.VMEM(weight.shape[1:], BF16) for weight in weights]
        weights = [in_hbm(weight) for weight in weights]
        scratch.append(pltpu.SemaphoreType.DMA((3, 4)))
    found = pl.pallas_call(
        functools.partial(experts_kernel, len(blocks), holds),
        out_shape=tuple(out_shape),
        in_specs=[vmem] * len(blocks) + [anywhere if holds else vmem] * 3,
        out_specs=tuple([vmem] * len(out_shape)),
        scratch_shapes=scratch,
        compiler_params=pltpu.CompilerParams(vmem_limit_bytes=VMEM_LIMIT),
        cost_estimate=pl.CostEstimate(
            flops=15 * 10**8, bytes_accessed=15 * 10**6, transcendentals=32768
        ),
        name=name,
    )(*blocks, *weights)
    return found[: len(blocks)], found[len(blocks) :]


def gather_rows(own):
    far = over_ctx(own, OPPOSITE)
    side = over_ctx(own, ACROSS)
    ahead = over_ctx(own, AHEAD)
    back = over_ctx(own, BACK)
    side_ahead = over_ctx(side, AHEAD)
    side_back = over_ctx(side, BACK)
    side_far = over_ctx(far, ACROSS)
    return (ahead, back, side), (far, side_ahead, side_back, side_far)


def added(*terms):
    total = terms[0].astype(F32)
    for term in terms[1:]:
        total = total + term.astype(F32)
    return total.astype(BF16)


def reduce_rows(own, near, far):
    ahead, back, side = near
    far, side_ahead, side_back, side_far = far
    side_far_in = over_ctx(side_far, ACROSS)
    side_ahead_in = over_ctx(side_ahead, BACK)
    side_back_in = over_ctx(side_back, AHEAD)
    side_in = over_ctx(added(side, side_ahead_in, side_back_in), ACROSS)
    far_in = over_ctx(added(far, side_far_in), OPPOSITE)
    ahead_in = over_ctx(ahead, BACK)
    back_in = over_ctx(back, AHEAD)
    return added(own, ahead_in, back_in, side_in, far_in)


def on_device(
    queries,
    prior_codes,
    fresh_codes,
    prior_powers,
    fresh_powers,
    block_mask,
    value_up,
    output_weight,
    residual,
    norm_gain,
    router,
    route_ids,
    gate_weight,
    up_weight,
    down_weight,
):
    core = lax.axis_index("exp") % CORES
    rows_block, head_count, key_width = queries.shape
    prior_blocks = prior_powers.shape[0]
    scales = power_two(jnp.concatenate([prior_powers, fresh_powers], axis=0))
    blocks_here = jnp.concatenate(
        [jnp.transpose(prior_codes), jnp.transpose(fresh_codes)], axis=1
    ).reshape(key_width, prior_blocks + 1, rows_block)
    blocks_here = jnp.transpose(blocks_here, (1, 0, 2)).astype(F32)
    blocks_here = (blocks_here * scales[:, None, None]).astype(BF16)
    near, far_blocks = gather_codes(blocks_here, core)
    groups = rows_block // 16
    split = queries.reshape(groups, 2, 8, head_count, key_width)
    first = jnp.where(core == 0, split[:, 0], split[:, 1])
    second = jnp.where(core == 0, split[:, 1], split[:, 0])
    ordered = jnp.stack([first, second], axis=0)
    ordered = jnp.transpose(ordered, (3, 0, 1, 2, 4)).reshape(head_count * rows_block, key_width)

    state = near_call(block_mask, ordered, near, value_up, output_weight)
    *state, done = state
    far = far_blocks(done)
    keep, send = far_call(block_mask, ordered, far, state, value_up)
    expert_count = router.shape[1]
    token_count, route_count = route_ids.shape
    capacity = token_count * route_count * 2 // expert_count
    route_hits = route_ids[:, :, None] == jnp.arange(expert_count)[None, None, :]
    flat_hits = route_hits.reshape(token_count * route_count, expert_count).astype(jnp.int32)
    before = jnp.cumsum(flat_hits, axis=0) - flat_hits
    slot_index = jnp.sum(before * flat_hits, axis=1)
    target = route_ids.reshape(-1) * capacity + slot_index
    placing = (target[None, :] == jnp.arange(expert_count * capacity)[:, None]).astype(BF16)
    placing_back = jnp.transpose(placing)
    gain = norm_gain.astype(F32)
    keep, send, placing, placing_back, route_ids, gain = lax.optimization_barrier(
        (keep, send, placing, placing_back, route_ids, gain)
    )
    paired = added(keep, core_swap(send))
    model_width = residual.shape[1]
    pieces = lax.all_to_all(
        paired.reshape(groups, 8, model_width),
        "exp",
        split_axis=0,
        concat_axis=0,
        tiled=True,
        axis_index_groups=SAME_CORE,
    )
    attention = jnp.sum(pieces.astype(F32), axis=0)
    hidden = (residual.astype(F32) + attention).astype(BF16)
    hidden_wide = hidden.astype(F32)
    normed = (
        hidden_wide
        * lax.rsqrt(jnp.mean(hidden_wide * hidden_wide, axis=1, keepdims=True) + 1e-06)
        * gain
    ).astype(BF16)
    affinity = jax.nn.sigmoid(jnp.dot(normed, router, preferred_element_type=F32))
    route_hits = route_ids[:, :, None] == jnp.arange(expert_count)[None, None, :]
    chosen = jnp.sum(jnp.where(route_hits, affinity[:, None, :], 0.0), axis=2)
    gate_values = 2.5 * chosen / jnp.sum(chosen, axis=1, keepdims=True)
    repeated = jnp.repeat(normed, route_count, axis=0)
    buffer = jnp.dot(placing, repeated, preferred_element_type=F32).astype(BF16)
    sectioned = lax.all_to_all(
        buffer.reshape(expert_count, capacity, model_width),
        "exp",
        split_axis=0,
        concat_axis=0,
        tiled=True,
    )
    own_rows = sectioned.reshape(expert_count * capacity, model_width)
    near_rows, far_rows = gather_rows(own_rows)
    near_terms, weights = experts_call(
        (own_rows,) + near_rows, (gate_weight, up_weight, down_weight), True, "experts_near"
    )
    far_terms, _ = experts_call(far_rows, weights, False, "experts_far")
    summed = reduce_rows(near_terms[0], near_terms[1:], far_terms)
    summed, gate_values, hidden = lax.optimization_barrier((summed, gate_values, hidden))
    returned = lax.all_to_all(
        summed.reshape(expert_count, capacity, model_width),
        "exp",
        split_axis=0,
        concat_axis=0,
        tiled=True,
    ).reshape(expert_count * capacity, model_width)
    gathered_back = jnp.dot(
        placing_back, returned, preferred_element_type=F32
    ).reshape(token_count, route_count, model_width)
    expert_mix = jnp.sum(gate_values[:, :, None] * gathered_back, axis=1)
    return (hidden.astype(F32) + expert_mix).astype(BF16)


def solution(mesh):
    in_specs = (
        P("ctx", "exp", None),
        P("ctx", None),
        P("ctx", None),
        P("ctx"),
        P("ctx"),
        P(),
        P("exp", None, None),
        P("exp", None),
        P(("ctx", "exp"), None),
        P(),
        P(),
        P(("ctx", "exp"), None),
        P("exp", None, "ctx"),
        P("exp", None, "ctx"),
        P("exp", "ctx", None),
    )
    out_specs = P(("ctx", "exp"), None)
    return jax.shard_map(
        on_device, mesh=mesh, in_specs=in_specs, out_specs=out_specs, check_vma=False
    )
```
